128 devices in a mesh: row: 16 (over y_lo, x, core), col: 8 (over z, y_hi).
Axes of the slice: x: 4, y: 4 (y_hi: 2, y_lo: 2; y = y_hi * 2 + y_lo), z: 4, core: 2. Of those that a mesh axis runs over, the one named last changes fastest.
Arguments:
- latent: bfloat16 [1, 128, 256, 640], P(None, 'row', 'col'), may hold values from -6 to 6
- timestep: int32 [1], replicated, may hold values from 0 to 499
- noise_seed: int32 [1], replicated, may hold values from 0 to 999999
- proj_seed: int32 [1], replicated, may hold values from 0 to 999999
- example_ids: int32 [1], replicated, may hold values from 0 to 99999
- time_weight: bfloat16 [640, 640], replicated, may hold values from -0.25 to 0.25
- conv1_weight: bfloat16 [5760, 640], replicated, may hold values from -0.078125 to 0.078125
- conv2_weight: bfloat16 [5760, 640], replicated, may hold values from -0.078125 to 0.078125
Outputs:
- section_out: bfloat16 [1, 128, 256, 640], P(None, 'row', 'col')
- sketch: float32 [1, 1024], replicated
The draws below stay inside these ranges and needn't reach their ends.
All inputs are finite; a program needn't handle non-finite values.
Results may differ from the reference program's by a relative error of at most 0.013.
Values may be sent and summed in bfloat16 or wider, within the bound.
A program may use at most 128 MiB of HBM per device.

```python
import math
import jax
import jax.numpy as jnp
from jax import lax

C = 640
K = 1024
EXAMPLES = 1
TH = 8
TW = 32
ROWS = 128
COLS = 256


def draw_latent(key, part):
    key = jax.random.fold_in(key, 7)
    keys = jax.random.split(key, 8)
    amp_lo = 0.8
    amp_hi = 1.6
    level_lo = -1.8
    noise = jax.random.normal(keys[0], (EXAMPLES, ROWS, COLS, C), jnp.float32)
    low_freq = math.log(1.0 / 128.0)
    high_freq = math.log(1.0 / 16.0)
    freq_row = jnp.exp(jax.random.uniform(keys[1], (3, C), jnp.float32, low_freq, high_freq))
    freq_col = jnp.exp(jax.random.uniform(keys[2], (3, C), jnp.float32, low_freq, high_freq))
    sign_row = (jax.random.randint(keys[3], (3, C), 0, 2) * 2 - 1).astype(jnp.float32)
    sign_col = (jax.random.randint(keys[4], (3, C), 0, 2) * 2 - 1).astype(jnp.float32)
    phases = jax.random.uniform(keys[5], (3, C), jnp.float32, 0.0, 2.0 * math.pi)
    amps = jax.random.uniform(keys[7], (3, C), jnp.float32, amp_lo, amp_hi)
    row_pos = jnp.arange(ROWS, dtype=jnp.float32)[:, None, None]
    col_pos = jnp.arange(COLS, dtype=jnp.float32)[None, :, None]
    field = jnp.zeros((ROWS, COLS, C), jnp.float32)
    for wave in range(3):
        angle = 2.0 * math.pi * (row_pos * (sign_row[wave] * freq_row[wave]) + col_pos * (sign_col[wave] * freq_col[wave])) + phases[wave]
        field = field + amps[wave] * jnp.sin(angle)
    level_key = jax.random.fold_in(key, 11)
    levels = jnp.exp(jax.random.uniform(level_key, (EXAMPLES, ROWS // TH, COLS // TW), jnp.float32, level_lo, 0.6))
    levels = jnp.repeat(jnp.repeat(levels, TH, axis=1), TW, axis=2)
    values = levels[:, :, :, None] * (field[None] + noise)
    return jnp.clip(values, -6.0, 6.0).astype(jnp.bfloat16)


def gaussian(rng, dims, deviation, limit, kind=jnp.bfloat16):
    result = jax.random.normal(rng, dims, jnp.float32) * deviation
    return jnp.minimum(jnp.maximum(result, -limit), limit).astype(kind)


def setup_inputs(seed: int = 0) -> dict:
    splits = jax.random.split(jax.random.key(seed), 9)
    return {
        "latent": draw_latent(jax.random.fold_in(splits[8], 71), 0),
        "timestep": jax.random.randint(splits[1], (EXAMPLES,), 0, 500).astype(jnp.int32),
        "noise_seed": jax.random.randint(splits[2], (1,), 0, 1000000).astype(jnp.int32),
        "proj_seed": jax.random.randint(splits[3], (1,), 0, 1000000).astype(jnp.int32),
        "example_ids": jax.random.randint(splits[4], (EXAMPLES,), 0, 100000).astype(jnp.int32),
        "time_weight": gaussian(splits[5], (C, C), C ** -0.5, 0.25),
        "conv1_weight": gaussian(splits[6], (9 * C, C), (9 * C) ** -0.5, 0.078125),
        "conv2_weight": gaussian(splits[7], (9 * C, C), (9 * C) ** -0.5, 0.078125),
    }


def mix_bits(value):
    value = value ^ lax.shift_right_logical(value, jnp.int32(16))
    value = value * jnp.int32(2146121005)
    value = value ^ lax.shift_right_logical(value, jnp.int32(15))
    value = value * jnp.int32(-2073254261)
    value = value ^ lax.shift_right_logical(value, jnp.int32(16))
    return value

def noise_field(example_ids, noise_seed, row_first, col_first, tile_rows, tile_cols, channels, rows_all, cols_all):
    row_ids = row_first + jnp.arange(tile_rows, dtype=jnp.int32)
    col_ids = col_first + jnp.arange(tile_cols, dtype=jnp.int32)
    chan_ids = jnp.arange(channels, dtype=jnp.int32)
    base = ((example_ids[:, None, None, None] * rows_all + row_ids[None, :, None, None]) * cols_all + col_ids[None, None, :, None]) * channels + chan_ids
    salt = mix_bits(noise_seed[0] + jnp.int32(0))
    total = jnp.zeros(base.shape, jnp.float32)
    for salt_index in range(4):
        bits = mix_bits(base * 4 + salt_index + salt)
        total = total + lax.shift_right_logical(bits, jnp.int32(8)).astype(jnp.float32) * (1.0 / 16777216.0)
    return (total - 2.0) * math.sqrt(3.0)

def plan(timestep):
    fraction = timestep.astype(jnp.float32) / 1000.0
    return jnp.cos((fraction + 0.008) / 1.008 * (math.pi / 2.0)) ** 2

def time_features(timestep, channels):
    half = channels // 2
    freqs = jnp.exp(-math.log(10000.0) * jnp.arange(half, dtype=jnp.float32) / half)
    angles = timestep.astype(jnp.float32)[:, None] * freqs[None, :]
    return jnp.concatenate([jnp.sin(angles), jnp.cos(angles)], axis=1)

def sign_block(first_index, width, proj_count, salt):
    flat_ids = first_index + jnp.arange(width, dtype=jnp.int32)
    column_ids = jnp.arange(proj_count, dtype=jnp.int32)
    bits = mix_bits(flat_ids[:, None] * proj_count + column_ids[None, :] + salt)
    return jnp.where(bits < 0, -1.0, 1.0).astype(jnp.float32)

def convolve(values, weight):
    kernel = weight.reshape(3, 3, C, C)
    return lax.conv_general_dilated(values, kernel, (1, 1), 'SAME', dimension_numbers=('NHWC', 'HWIO', 'NHWC'), preferred_element_type=jnp.float32)

def reference(latent, timestep, noise_seed, proj_seed, example_ids, time_weight, conv1_weight, conv2_weight):
    noise = noise_field(example_ids, noise_seed, 0, 0, ROWS, COLS, C, ROWS, COLS)
    abar = plan(timestep)[:, None, None, None]
    noisy = (jnp.sqrt(abar) * latent.astype(jnp.float32) + jnp.sqrt(1.0 - abar) * noise).astype(jnp.bfloat16)
    act = jax.nn.silu(noisy.astype(jnp.float32)).astype(jnp.bfloat16)
    features = time_features(timestep, C).astype(jnp.bfloat16)
    temb = jnp.dot(features, time_weight, preferred_element_type=jnp.float32)
    pre = convolve(act, conv1_weight) + temb[:, None, None, :]
    hidden = jax.nn.silu(pre).astype(jnp.bfloat16)
    out_full = noisy.astype(jnp.float32) + convolve(hidden, conv2_weight)
    section_out = out_full.astype(jnp.bfloat16)
    cot = ((out_full - noise) / math.sqrt(ROWS * COLS)).astype(jnp.bfloat16).astype(jnp.float32)
    padded = jnp.pad(hidden, ((0, 0), (1, 1), (1, 1), (0, 0)))
    pieces = []
    for row_off in range(3):
        for col_off in range(3):
            shifted = padded[:, row_off:row_off + ROWS, col_off:col_off + COLS, :].astype(jnp.float32)
            pieces.append(jnp.einsum('brco,brci->boi', cot, shifted))
    grad = jnp.stack(pieces, axis=2).reshape(EXAMPLES, C, 9 * C)
    salt = mix_bits(proj_seed[0] + jnp.int32(12345))

    def accumulate(total, inputs):
        out_chan, rows_now = inputs
        block = sign_block(out_chan * (9 * C), 9 * C, K, salt)
        return (total + jnp.dot(rows_now, block, preferred_element_type=jnp.float32, precision=lax.Precision.HIGHEST), None)
    start = jnp.zeros((EXAMPLES, K), jnp.float32)
    total, _ = lax.scan(accumulate, start, (jnp.arange(C, dtype=jnp.int32), jnp.transpose(grad, (1, 0, 2))))
    sketch = total / math.sqrt(9.0 * C * C)
    return (section_out, sketch)
```

```python
import functools
import math

import jax
import jax.numpy as jnp
from jax import lax
from jax.experimental import pallas as pl
from jax.experimental.pallas import tpu as pltpu
from jax.sharding import PartitionSpec as P

K = 1024
M1 = 2146121005
M2 = -2073254261
MESH = pl.DeviceIdType.MESH


def wrap32(value):
    value &= 0xFFFFFFFF
    return value - (1 << 32) if value >= (1 << 31) else value


def extended(cells, sides, width):
    for axis, dim in sides:
        count = lax.axis_size(axis)
        ends = count - 1
        head = lax.slice_in_dim(cells, 0, width, axis=dim)
        tail = lax.slice_in_dim(cells, cells.shape[dim] - width, cells.shape[dim], axis=dim)
        cells = jnp.concatenate(
            [
                lax.ppermute(tail, axis, [(i, (i + 1) % count) for i in range(ends)]),
                cells,
                lax.ppermute(head, axis, [((i + 1) % count, i) for i in range(ends)]),
            ],
            axis=dim,
        )
    return cells


def mix_bits(value):
    value = value ^ lax.shift_right_logical(value, jnp.int32(16))
    value = value * jnp.int32(M1)
    value = value ^ lax.shift_right_logical(value, jnp.int32(15))
    value = value * jnp.int32(M2)
    value = value ^ lax.shift_right_logical(value, jnp.int32(16))
    return value


def noise_field(
    example_ids, noise_seed, row_first, col_first, tile_rows, tile_cols, channels, rows_all, cols_all
):
    row_ids = row_first + jnp.arange(tile_rows, dtype=jnp.int32)
    col_ids = col_first + jnp.arange(tile_cols, dtype=jnp.int32)
    chan_ids = jnp.arange(channels, dtype=jnp.int32)
    base = (
        (example_ids[:, None, None, None] * rows_all + row_ids[None, :, None, None]) * cols_all
        + col_ids[None, None, :, None]
    ) * channels + chan_ids
    salt = mix_bits(noise_seed[0])
    total = jnp.zeros(base.shape, jnp.float32)
    for salt_index in range(4):
        bits = mix_bits(base * 4 + salt_index + salt)
        total = total + lax.shift_right_logical(bits, jnp.int32(8)).astype(jnp.float32) * (
            1.0 / 16777216.0
        )
    return (total - 2.0) * math.sqrt(3.0)


def plan(timestep):
    fraction = timestep.astype(jnp.float32) / 1000.0
    return jnp.cos((fraction + 0.008) / 1.008 * (math.pi / 2.0)) ** 2


def time_features(timestep, channels):
    half = channels // 2
    freqs = jnp.exp(-math.log(10000.0) * jnp.arange(half, dtype=jnp.float32) / half)
    angles = timestep.astype(jnp.float32)[:, None] * freqs[None, :]
    return jnp.concatenate([jnp.sin(angles), jnp.cos(angles)], axis=1)


CH = 640
TAPS = 9 * CH
THIRD = 3 * CH
CUT = 1024
OWN = 5
RUN = OWN * TAPS
PADDED = 29184
BLOCK = 1536
ORDERS = (("x", "y", "z"), ("y", "z", "x"), ("z", "x", "y"))


def place():
    r = lax.axis_index("row")
    c = lax.axis_index("col")
    return {
        "core": lax.rem(r, 2),
        "x": lax.rem(r // 2, 4),
        "y": lax.rem(c, 2) * 2 + r // 8,
        "z": c // 2,
    }


def device(at, **moved):
    at = {**at, **moved}
    row = (lax.rem(at["y"], 2) * 4 + at["x"]) * 2 + at["core"]
    return (row, at["z"] * 2 + at["y"] // 2)


def hop(at, axis, by):
    return lax.rem(at[axis] + (by + 4), 4)


def peers_of(at):
    out = []
    for step in range(4):
        for flip in range(2):
            if step or flip:
                out.append(device(at, x=hop(at, "x", step), core=lax.rem(at["core"] + flip, 2)))
    for axis in ("y", "z"):
        for step in range(1, 4):
            out.append(device(at, **{axis: hop(at, axis, step)}))
    return out


def selection(third, core):
    row = lax.broadcasted_iota(jnp.int32, (320, CH), 0)
    owner = lax.shift_right_logical(row * 52429, jnp.int32(18))
    channel = row - owner * OWN
    digits = (lax.shift_right_logical(owner, jnp.int32(4)), lax.shift_right_logical(owner, jnp.int32(2)) & 3, owner & 3)
    named = dict(zip(ORDERS[third], digits))
    wanted = ((core * 4 + named["x"]) * 4 + named["y"]) * 4 + named["z"]
    wanted = wanted * OWN + channel
    lane = lax.broadcasted_iota(jnp.int32, (320, CH), 1)
    return jnp.where(lane == wanted, 1.0, 0.0).astype(jnp.bfloat16)


def f32(value):
    return value.astype(jnp.float32)


def project(salt, first, row, grow, acc):
    q = lax.shift_right_logical(salt, jnp.int32(10))
    s = salt & (K - 1)
    m_first = (first + q) & jnp.int32((1 << 22) - 1)
    ahead = m_first & 255
    h_first = lax.shift_right_logical(m_first - ahead, jnp.int32(6))
    flat = row[...]
    whole = jnp.sum(flat)
    one = pltpu.roll(flat, ahead, axis=1)
    two = pltpu.roll(one, 1, axis=1)
    one_hi = one.astype(jnp.bfloat16)
    two_hi = two.astype(jnp.bfloat16)
    one_lo = (one - f32(one_hi)).astype(jnp.bfloat16)
    two_lo = (two - f32(two_hi)).astype(jnp.bfloat16)
    none = jnp.zeros((4, PADDED), jnp.bfloat16)
    grow[...] = jnp.concatenate([one_hi, two_hi, one_lo, two_lo, none], axis=0)
    acc[...] = jnp.zeros_like(acc)
    j = lax.broadcasted_iota(jnp.int32, (1, K), 1)
    m_row = lax.broadcasted_iota(jnp.int32, (64, 1), 0)

    def body(step, carry):
        h_block = h_first + step * (BLOCK // 64)
        parts = []
        for part in range(BLOCK // 64):
            if part % 4 == 0:
                h_four = (h_block + part) & 65535
                column = (m_row ^ lax.shift_right_logical(h_four, jnp.int32(10))) * jnp.int32(
                    wrap32(1024 * M1)
                )
            h = h_four + part % 4
            line = (j ^ (h & 1023)) * jnp.int32(M1) + h * jnp.int32(wrap32(65536 * M1))
            w = line + column
            y = (w ^ lax.shift_right_logical(w, jnp.int32(15))) * jnp.int32(M2)
            parts.append(jnp.where(y < 0, 1.0, 0.0).astype(jnp.bfloat16))
        signs = jnp.concatenate(parts, axis=0)
        lanes = pl.ds(pl.multiple_of(step * BLOCK, BLOCK), BLOCK)
        acc[...] += jnp.dot(grow[:, lanes], signs, preferred_element_type=jnp.float32)
        return carry

    lax.fori_loop(0, PADDED // BLOCK, body, 0)
    here = whole - 2.0 * (acc[0:1, :] + acc[2:3, :])
    past = whole - 2.0 * (acc[1:2, :] + acc[3:4, :])
    return pltpu.roll(jnp.where(j >= s, here, past), (K - s) & (K - 1), axis=1)


def back_kernel(
    salt_ref, cot_ref, hid_ref, out_ref,
    cot_far, hid_far, lhs, s1, r1a, r1b, r1, f2, s2, r2a, r2b, r2, f3, r3, row, grow, acc,
    sum8, sum4, sum4b,
    pair_send, pair_recv, ring_send, ring_recv, tail_send, tail_recv, all_send, all_recv,
):
    at = place()
    peers = peers_of(at)
    barrier = pltpu.get_barrier_semaphore()
    for peer in peers:
        pl.semaphore_signal(barrier, inc=1, device_id=peer, device_id_type=MESH)
    pl.semaphore_wait(barrier, len(peers))

    def send(src, dst, send_sem, recv_sem, to):
        copy = pltpu.make_async_remote_copy(
            src_ref=src, dst_ref=dst, send_sem=send_sem, recv_sem=recv_sem,
            device_id=to, device_id_type=MESH,
        )
        copy.start()
        return copy

    partner = device(at, core=lax.rem(at["core"] + 1, 2))
    pair = [
        send(cot_ref, cot_far, pair_send.at[0], pair_recv.at[0], partner),
        send(hid_ref, hid_far, pair_send.at[1], pair_recv.at[1], partner),
    ]
    pair[0].wait_recv()
    for third in range(3):
        pick = selection(third, at["core"])
        for side, cot in enumerate((cot_ref, cot_far)):
            lhs[third, side] = lax.dot_general(
                pick, cot[...], (((1,), (1,)), ((), ())), preferred_element_type=jnp.float32
            ).astype(jnp.bfloat16)
    pair[1].wait_recv()

    def ring_one(third, level, blocks, ra, rb):
        axis = ORDERS[third][level]
        mine = at[axis]
        up = device(at, **{axis: hop(at, axis, 1)})
        down = device(at, **{axis: hop(at, axis, -1)})
        across = hop(at, axis, 2)
        sems = (third, level)
        return [
            send(blocks.at[third, across, :, pl.ds(0, CUT)], ra.at[third],
                 ring_send.at[third, level, 0], ring_recv.at[third, level, 0], up),
            send(blocks.at[third, across, :, pl.ds(CUT, THIRD - CUT)], rb.at[third],
                 ring_send.at[third, level, 1], ring_recv.at[third, level, 1], down),
        ]

    def ring_two(third, level, blocks, ra, rb, first, landed):
        axis = ORDERS[third][level]
        above = hop(at, axis, 1)
        below = hop(at, axis, -1)
        first[0].wait_recv()
        old = blocks[third, above, :, 0:CUT]
        blocks[third, above, :, 0:CUT] = (f32(old) + f32(ra[third])).astype(jnp.bfloat16)
        up = send(blocks.at[third, above], landed.at[third, 0],
                  ring_send.at[third, level, 2], ring_recv.at[third, level, 2],
                  device(at, **{axis: above}))
        first[1].wait_recv()
        old = blocks[third, below, :, CUT:THIRD]
        blocks[third, below, :, CUT:THIRD] = (f32(old) + f32(rb[third])).astype(jnp.bfloat16)
        down = send(blocks.at[third, below], landed.at[third, 1],
                    ring_send.at[third, level, 3], ring_recv.at[third, level, 3],
                    device(at, **{axis: below}))
        return [up, down]

    started = list(pair)
    ones = []
    for third in range(3):
        for dx in range(3):
            near = hid_ref[dx, third : third + 8].reshape(256, CH)
            far = hid_far[dx, third : third + 8].reshape(256, CH)
            total = jnp.dot(lhs[third, 0], near, preferred_element_type=jnp.float32)
            total += jnp.dot(lhs[third, 1], far, preferred_element_type=jnp.float32)
            s1[third, :, :, dx * CH : (dx + 1) * CH] = total.astype(jnp.bfloat16).reshape(4, 80, CH)
        ones.append(ring_one(third, 0, s1, r1a, r1b))
    twos = [ring_two(t, 0, s1, r1a, r1b, ones[t], r1) for t in range(3)]
    started += [copy for group in ones + twos for copy in group]
    ones = []
    for third in range(3):
        mine = at[ORDERS[third][0]]
        for copy in twos[third]:
            copy.wait_recv()
        total = f32(s1[third, mine]) + f32(r1[third, 0]) + f32(r1[third, 1])
        for block in range(4):
            piece = total[block * 20 : block * 20 + 20]
            f2[third, block, 0:20] = piece
            s2[third, block] = jnp.concatenate([piece, jnp.zeros((12, THIRD), jnp.float32)], axis=0).astype(
                jnp.bfloat16
            )
        ones.append(ring_one(third, 1, s2, r2a, r2b))
    twos = [ring_two(t, 1, s2, r2a, r2b, ones[t], r2) for t in range(3)]
    started += [copy for group in ones + twos for copy in group]
    lasts = []
    for third in range(3):
        mine = at[ORDERS[third][1]]
        for copy in twos[third]:
            copy.wait_recv()
        total = f2[third, mine, 0:20] + f32(r2[third, 0, 0:20]) + f32(r2[third, 1, 0:20])
        for block in range(4):
            f3[third, block] = jnp.concatenate(
                [total[block * OWN : (block + 1) * OWN], jnp.zeros((3, THIRD), jnp.float32)], axis=0
            )
        axis = ORDERS[third][2]
        group = []
        for step in range(1, 4):
            to = hop(at, axis, step)
            group.append(
                send(f3.at[third, to], r3.at[third, step - 1],
                     tail_send.at[third, step - 1], tail_recv.at[third, step - 1],
                     device(at, **{axis: to}))
            )
        lasts.append(group)
    row[...] = jnp.zeros_like(row)
    for third in range(3):
        mine = at[ORDERS[third][2]]
        for copy in lasts[third]:
            copy.wait_recv()
        started += lasts[third]
        total = f3[third, mine] + r3[third, 0] + r3[third, 1] + r3[third, 2]
        for channel in range(OWN):
            lanes = pl.ds(channel * TAPS + third * THIRD, THIRD)
            row[0:1, lanes] = total[channel : channel + 1]

    owner = ((at["core"] * 4 + at["x"]) * 4 + at["y"]) * 4 + at["z"]
    share = project(salt_ref[0], owner * RUN, row, grow, acc)

    share = share * (1.0 / math.sqrt(9.0 * CH * CH))
    me = at["x"] * 2 + at["core"]
    sum8[me] = share
    group = []
    for index, peer in enumerate(peers[:7]):
        group.append(send(sum8.at[me], sum8.at[me], all_send.at[index], all_recv.at[index], peer))
    for copy in group:
        copy.wait_recv()
    started += group
    share = sum8[0]
    for index in range(1, 8):
        share = share + sum8[index]
    for axis, slots, base in (("y", sum4, 7), ("z", sum4b, 10)):
        me = at[axis]
        slots[me] = share
        group = []
        for index in range(3):
            group.append(send(slots.at[me], slots.at[me], all_send.at[base + index],
                              all_recv.at[base + index], peers[base + index]))
        for copy in group:
            copy.wait_recv()
        started += group
        share = slots[0] + slots[1] + slots[2] + slots[3]
    out_ref[...] = share
    for copy in started:
        copy.wait_send()


def back(salt, cot, hid):
    bf16, full = jnp.bfloat16, jnp.float32
    vmem = pltpu.VMEM
    dma = pltpu.SemaphoreType.DMA
    return pl.pallas_call(
        back_kernel,
        out_shape=jax.ShapeDtypeStruct((1, K), full),
        in_specs=[
            pl.BlockSpec(memory_space=pltpu.SMEM),
            pl.BlockSpec(memory_space=pltpu.VMEM),
            pl.BlockSpec(memory_space=pltpu.VMEM),
        ],
        out_specs=pl.BlockSpec(memory_space=pltpu.VMEM),
        scratch_shapes=[
            vmem((256, CH), bf16),
            vmem((3, 10, 32, CH), bf16),
            vmem((3, 2, 320, 256), bf16),
            vmem((3, 4, 80, THIRD), bf16),
            vmem((3, 80, CUT), bf16),
            vmem((3, 80, THIRD - CUT), bf16),
            vmem((3, 2, 80, THIRD), bf16),
            vmem((3, 4, 24, THIRD), full),
            vmem((3, 4, 32, THIRD), bf16),
            vmem((3, 32, CUT), bf16),
            vmem((3, 32, THIRD - CUT), bf16),
            vmem((3, 2, 32, THIRD), bf16),
            vmem((3, 4, 8, THIRD), full),
            vmem((3, 3, 8, THIRD), full),
            vmem((1, PADDED), full),
            vmem((8, PADDED), bf16),
            vmem((8, K), full),
            vmem((8, 1, K), full),
            vmem((4, 1, K), full),
            vmem((4, 1, K), full),
            dma((2,)), dma((2,)),
            dma((3, 2, 4)), dma((3, 2, 4)),
            dma((3, 3)), dma((3, 3)),
            dma((13,)), dma((13,)),
        ],
        compiler_params=pltpu.CompilerParams(
            collective_id=0, has_side_effects=True, vmem_limit_bytes=56 * 2**20
        ),
    )(salt, cot, hid)


def unfold(padded, tile_rows, tile_cols):
    pieces = []
    for row_off in range(3):
        for col_off in range(3):
            pieces.append(
                padded[:, row_off : row_off + tile_rows, col_off : col_off + tile_cols, :]
            )
    joined = jnp.concatenate(pieces, axis=3)
    return joined.reshape(joined.shape[0], tile_rows * tile_cols, joined.shape[3])


def on_device(
    latent, timestep, noise_seed, proj_seed, example_ids, time_weight, conv1_weight, conv2_weight
):
    batch, tile_rows, tile_cols, channels = latent.shape
    rows_count = lax.axis_size("row")
    cols_count = lax.axis_size("col")
    rows_all = tile_rows * rows_count
    cols_all = tile_cols * cols_count
    row_first = lax.axis_index("row") * tile_rows
    col_first = lax.axis_index("col") * tile_cols
    noise = noise_field(
        example_ids, noise_seed, row_first, col_first, tile_rows, tile_cols, channels, rows_all, cols_all
    )
    abar = plan(timestep)[:, None, None, None]
    noisy = (jnp.sqrt(abar) * latent.astype(jnp.float32) + jnp.sqrt(1.0 - abar) * noise).astype(
        jnp.bfloat16
    )
    act = jax.nn.silu(noisy.astype(jnp.float32)).astype(jnp.bfloat16)
    act_pad = extended(act, (("row", 1), ("col", 2)), 1)
    features = time_features(timestep, channels).astype(jnp.bfloat16)
    temb = jnp.dot(features, time_weight, preferred_element_type=jnp.float32)
    act_cols = unfold(act_pad, tile_rows, tile_cols).reshape(
        batch * tile_rows * tile_cols, 9 * channels
    )
    pre = jnp.dot(act_cols, conv1_weight, preferred_element_type=jnp.float32).reshape(
        batch, tile_rows, tile_cols, channels
    )
    hidden = jax.nn.silu(pre + temb[:, None, None, :]).astype(jnp.bfloat16)
    hid_pad = extended(hidden, (("row", 1), ("col", 2)), 1)
    hid_cols = unfold(hid_pad, tile_rows, tile_cols)
    conv_out = jnp.dot(
        hid_cols.reshape(batch * tile_rows * tile_cols, 9 * channels),
        conv2_weight,
        preferred_element_type=jnp.float32,
    )
    out_full = noisy.astype(jnp.float32) + conv_out.reshape(batch, tile_rows, tile_cols, channels)
    section_out = out_full.astype(jnp.bfloat16)
    cot = ((out_full - noise) / math.sqrt(rows_all * cols_all)).astype(jnp.bfloat16)
    cot = cot.reshape(batch * tile_rows * tile_cols, channels)
    shifted = jnp.stack([hid_pad[0, :, dx : dx + tile_cols, :] for dx in range(3)])
    salt = mix_bits(proj_seed + jnp.int32(12345))
    sketch = back(salt, cot, shifted)
    return (section_out, sketch)


def solution(mesh):
    placed = (P(None, "row", "col", None), P(), P(), P(), P(), P(), P(), P())
    return jax.shard_map(
        on_device,
        mesh=mesh,
        in_specs=placed,
        out_specs=(P(None, "row", "col", None), P()),
        check_vma=False,
    )
```

```python
import functools
import math

import jax
import jax.numpy as jnp
from jax import lax
from jax.experimental import pallas as pl
from jax.experimental.pallas import tpu as pltpu
from jax.sharding import PartitionSpec as P

K = 1024
FILLS = (8, 16, 36, 10, 18)
M1 = 2146121005
M2 = -2073254261
MESH = pl.DeviceIdType.MESH


def wrap32(value):
    value &= 0xFFFFFFFF
    return value - (1 << 32) if value >= (1 << 31) else value


def extended(cells, sides, width):
    for axis, dim in sides:
        count = lax.axis_size(axis)
        ends = count - 1
        head = lax.slice_in_dim(cells, 0, width, axis=dim)
        tail = lax.slice_in_dim(cells, cells.shape[dim] - width, cells.shape[dim], axis=dim)
        cells = jnp.concatenate(
            [
                lax.ppermute(tail, axis, [(i, (i + 1) % count) for i in range(ends)]),
                cells,
                lax.ppermute(head, axis, [((i + 1) % count, i) for i in range(ends)]),
            ],
            axis=dim,
        )
    return cells


def mix_bits(value):
    value = value ^ lax.shift_right_logical(value, jnp.int32(16))
    value = value * jnp.int32(M1)
    value = value ^ lax.shift_right_logical(value, jnp.int32(15))
    value = value * jnp.int32(M2)
    value = value ^ lax.shift_right_logical(value, jnp.int32(16))
    return value


def noise_field(
    example_ids, noise_seed, row_first, col_first, tile_rows, tile_cols, channels, rows_all, cols_all
):
    row_ids = row_first + jnp.arange(tile_rows, dtype=jnp.int32)
    col_ids = col_first + jnp.arange(tile_cols, dtype=jnp.int32)
    chan_ids = jnp.arange(channels, dtype=jnp.int32)
    base = (
        (example_ids[:, None, None, None] * rows_all + row_ids[None, :, None, None]) * cols_all
        + col_ids[None, None, :, None]
    ) * channels + chan_ids
    salt = mix_bits(noise_seed[0])
    total = jnp.zeros(base.shape, jnp.float32)
    for salt_index in range(4):
        bits = mix_bits(base * 4 + salt_index + salt)
        total = total + lax.shift_right_logical(bits, jnp.int32(8)).astype(jnp.float32) * (
            1.0 / 16777216.0
        )
    return (total - 2.0) * math.sqrt(3.0)


def plan(timestep):
    fraction = timestep.astype(jnp.float32) / 1000.0
    return jnp.cos((fraction + 0.008) / 1.008 * (math.pi / 2.0)) ** 2


def time_features(timestep, channels):
    half = channels // 2
    freqs = jnp.exp(-math.log(10000.0) * jnp.arange(half, dtype=jnp.float32) / half)
    angles = timestep.astype(jnp.float32)[:, None] * freqs[None, :]
    return jnp.concatenate([jnp.sin(angles), jnp.cos(angles)], axis=1)


CH = 640
TAPS = 9 * CH
THIRD = 3 * CH
CUT = 1024
OWN = 5
RUN = OWN * TAPS
PADDED = 29184
BLOCK = 4864
F8 = jnp.float8_e4m3fn
PARTS = 4
ORDERS = (("x", "y", "z"), ("y", "z", "x"), ("z", "x", "y"))


def place():
    r = lax.axis_index("row")
    c = lax.axis_index("col")
    return {
        "core": lax.rem(r, 2),
        "x": lax.rem(r // 2, 4),
        "y": lax.rem(c, 2) * 2 + r // 8,
        "z": c // 2,
    }


def device(at, **moved):
    at = {**at, **moved}
    row = (lax.rem(at["y"], 2) * 4 + at["x"]) * 2 + at["core"]
    return (row, at["z"] * 2 + at["y"] // 2)


def hop(at, axis, by):
    return lax.rem(at[axis] + (by + 4), 4)


def peers_of(at):
    out = []
    for step in range(4):
        for flip in range(2):
            if step or flip:
                out.append(device(at, x=hop(at, "x", step), core=lax.rem(at["core"] + flip, 2)))
    for axis in ("y", "z"):
        for step in range(1, 4):
            out.append(device(at, **{axis: hop(at, axis, step)}))
    return out


def selection(third, core):
    row = lax.broadcasted_iota(jnp.int32, (320, 1), 0)
    owner = lax.shift_right_logical(row * 52429, jnp.int32(18))
    channel = row - owner * OWN
    digits = (lax.shift_right_logical(owner, jnp.int32(4)), lax.shift_right_logical(owner, jnp.int32(2)) & 3, owner & 3)
    named = dict(zip(ORDERS[third], digits))
    wanted = ((core * 4 + named["x"]) * 4 + named["y"]) * 4 + named["z"]
    wanted = wanted * OWN + channel
    lane = lax.broadcasted_iota(jnp.int32, (320, CH), 1)
    return jnp.where(lane == wanted, 1.0, 0.0).astype(jnp.bfloat16)


def f32(value):
    return value.astype(jnp.float32)


def shift_right(value, by):
    return lax.shift_right_logical(value, jnp.int32(by))


def alignment(salt, first):
    m_first = (first + shift_right(salt, 10)) & jnp.int32((1 << 22) - 1)
    ahead = m_first & 255
    return ahead, shift_right(m_first - ahead, 6)


def make_signs(salt, first, bits, low, high):
    h_first = alignment(salt, first)[1]
    lane = lax.broadcasted_iota(jnp.int32, (1, 128), 1)
    m_row = lax.broadcasted_iota(jnp.int32, (32, 128), 0)

    def body(step, carry):
        h_four = (h_first + step * 4) & 65535
        high_bits = shift_right(h_four, 10)
        columns = [((m_row + half) ^ high_bits) * jnp.int32(wrap32(1024 * M1)) for half in (0, 32)]
        for part in range(4):
            h = h_four + part
            for j in range(0, K, 128):
                line = ((lane + j) ^ (h & 1023)) * jnp.int32(M1) + h * jnp.int32(wrap32(65536 * M1))
                line = jnp.broadcast_to(line, (32, 128))
                for half in range(2):
                    w = line + columns[half]
                    y = (w ^ shift_right(w, 15)) * jnp.int32(M2)
                    rows = pl.ds(pl.multiple_of(step * 256 + part * 64 + half * 32, 32), 32)
                    bits[rows, j : j + 128] = lax.shift_right_arithmetic(y, 31).astype(jnp.int8).astype(F8)
        return carry

    lax.fori_loop(low, high, body, 0)


def project(salt, first, row, grow, bits, acc):
    s = salt & (K - 1)
    ahead = alignment(salt, first)[0]
    flat = row[...]
    whole = jnp.sum(flat)
    largest = jnp.maximum(jnp.max(jnp.abs(flat)), 1e-30)
    one = pltpu.roll(flat * (16.0 / largest), ahead, axis=1)
    two = pltpu.roll(one, 1, axis=1)
    for block in range(PADDED // BLOCK):
        lanes = slice(block * BLOCK, (block + 1) * BLOCK)
        pair = jnp.concatenate([one[:, lanes], two[:, lanes]], axis=0)
        pieces = []
        for _ in range(PARTS):
            piece = lax.round(pair, lax.RoundingMethod.TO_NEAREST_EVEN)
            pieces.append(piece)
            pair = (pair - piece) * 32.0
        pieces.append(jnp.zeros((24, BLOCK), jnp.float32))
        grow[:, lanes] = jnp.concatenate(pieces, axis=0).astype(F8)
    acc[...] = jnp.zeros_like(acc)

    def body(step, carry):
        lanes = pl.ds(pl.multiple_of(step * BLOCK, BLOCK), BLOCK)
        acc[...] += jnp.dot(grow[:, lanes], bits[lanes, :], preferred_element_type=jnp.float32)
        return carry

    lax.fori_loop(0, PADDED // BLOCK, body, 0)
    total = acc[6:8, :]
    for index in (2, 1, 0):
        total = acc[2 * index : 2 * index + 2, :] + total * (1.0 / 32.0)
    total = whole + total * (largest * (2.0 / 16.0))
    j = lax.broadcasted_iota(jnp.int32, (1, K), 1)
    return pltpu.roll(jnp.where(j >= s, total[0:1], total[1:2]), (K - s) & (K - 1), axis=1)


def back_kernel(
    salt_ref, cot_ref, hid_ref, out_ref,
    cot_far, hid_far, lhs, s1, r1a, r1b, r1, f2, s2, r2a, r2b, r2, f3, r3, row, grow, acc, bits,
    sum8, sum4, sum4b,
    pair_send, pair_recv, ring_send, ring_recv, tail_send, tail_recv, all_send, all_recv,
):
    at = place()
    peers = peers_of(at)
    barrier = pltpu.get_barrier_semaphore()
    for peer in peers:
        pl.semaphore_signal(barrier, inc=1, device_id=peer, device_id_type=MESH)
    pl.semaphore_wait(barrier, len(peers))

    def send(src, dst, send_sem, recv_sem, to):
        copy = pltpu.make_async_remote_copy(
            src_ref=src, dst_ref=dst, send_sem=send_sem, recv_sem=recv_sem,
            device_id=to, device_id_type=MESH,
        )
        copy.start()
        return copy

    salt = salt_ref[0]
    owner = ((at["core"] * 4 + at["x"]) * 4 + at["y"]) * 4 + at["z"]
    marks = [0]

    def fill(count):
        low = marks[-1]
        high = min(low + count, PADDED // 256)
        marks.append(high)
        if high > low:
            make_signs(salt, owner * RUN, bits, low, high)

    partner = device(at, core=lax.rem(at["core"] + 1, 2))
    pair = [
        send(cot_ref, cot_far, pair_send.at[0], pair_recv.at[0], partner),
        send(hid_ref, hid_far, pair_send.at[1], pair_recv.at[1], partner),
    ]
    fill(FILLS[0])
    pair[0].wait_recv()
    for third in range(3):
        pick = selection(third, at["core"])
        for side, cot in enumerate((cot_ref, cot_far)):
            lhs[third, side] = lax.dot_general(
                pick, cot[...], (((1,), (1,)), ((), ())), preferred_element_type=jnp.float32
            ).astype(jnp.bfloat16)
    pair[1].wait_recv()

    def ring_one(third, level, blocks, ra, rb):
        axis = ORDERS[third][level]
        mine = at[axis]
        up = device(at, **{axis: hop(at, axis, 1)})
        down = device(at, **{axis: hop(at, axis, -1)})
        across = hop(at, axis, 2)
        sems = (third, level)
        return [
            send(blocks.at[third, across, :, pl.ds(0, CUT)], ra.at[third],
                 ring_send.at[third, level, 0], ring_recv.at[third, level, 0], up),
            send(blocks.at[third, across, :, pl.ds(CUT, THIRD - CUT)], rb.at[third],
                 ring_send.at[third, level, 1], ring_recv.at[third, level, 1], down),
        ]

    def ring_two(third, level, blocks, ra, rb, first, landed):
        axis = ORDERS[third][level]
        above = hop(at, axis, 1)
        below = hop(at, axis, -1)
        first[0].wait_recv()
        old = blocks[third, above, :, 0:CUT]
        blocks[third, above, :, 0:CUT] = (f32(old) + f32(ra[third])).astype(jnp.bfloat16)
        up = send(blocks.at[third, above], landed.at[third, 0],
                  ring_send.at[third, level, 2], ring_recv.at[third, level, 2],
                  device(at, **{axis: above}))
        first[1].wait_recv()
        old = blocks[third, below, :, CUT:THIRD]
        blocks[third, below, :, CUT:THIRD] = (f32(old) + f32(rb[third])).astype(jnp.bfloat16)
        down = send(blocks.at[third, below], landed.at[third, 1],
                    ring_send.at[third, level, 3], ring_recv.at[third, level, 3],
                    device(at, **{axis: below}))
        return [up, down]

    started = list(pair)
    ones = []
    for third in range(3):
        for dx in range(3):
            near = hid_ref[dx, third : third + 8].reshape(256, CH)
            far = hid_far[dx, third : third + 8].reshape(256, CH)
            total = jnp.dot(lhs[third, 0], near, preferred_element_type=jnp.float32)
            total += jnp.dot(lhs[third, 1], far, preferred_element_type=jnp.float32)
            s1[third, :, :, dx * CH : (dx + 1) * CH] = total.astype(jnp.bfloat16).reshape(4, 80, CH)
        ones.append(ring_one(third, 0, s1, r1a, r1b))
    fill(FILLS[1])
    twos = [ring_two(t, 0, s1, r1a, r1b, ones[t], r1) for t in range(3)]
    started += [copy for group in ones + twos for copy in group]
    fill(FILLS[2])
    ones = []
    for third in range(3):
        mine = at[ORDERS[third][0]]
        for copy in twos[third]:
            copy.wait_recv()
        total = f32(s1[third, mine]) + f32(r1[third, 0]) + f32(r1[third, 1])
        for block in range(4):
            piece = total[block * 20 : block * 20 + 20]
            f2[third, block, 0:20] = piece
            s2[third, block] = jnp.concatenate([piece, jnp.zeros((12, THIRD), jnp.float32)], axis=0).astype(
                jnp.bfloat16
            )
        ones.append(ring_one(third, 1, s2, r2a, r2b))
    fill(FILLS[3])
    twos = [ring_two(t, 1, s2, r2a, r2b, ones[t], r2) for t in range(3)]
    started += [copy for group in ones + twos for copy in group]
    fill(FILLS[4])
    lasts = []
    for third in range(3):
        mine = at[ORDERS[third][1]]
        for copy in twos[third]:
            copy.wait_recv()
        total = f2[third, mine, 0:20] + f32(r2[third, 0, 0:20]) + f32(r2[third, 1, 0:20])
        for block in range(4):
            f3[third, block] = jnp.concatenate(
                [total[block * OWN : (block + 1) * OWN], jnp.zeros((3, THIRD), jnp.float32)], axis=0
            )
        axis = ORDERS[third][2]
        group = []
        for step in range(1, 4):
            to = hop(at, axis, step)
            group.append(
                send(f3.at[third, to], r3.at[third, step - 1],
                     tail_send.at[third, step - 1], tail_recv.at[third, step - 1],
                     device(at, **{axis: to}))
            )
        lasts.append(group)
    fill(PADDED)
    row[...] = jnp.zeros_like(row)
    for third in range(3):
        mine = at[ORDERS[third][2]]
        for copy in lasts[third]:
            copy.wait_recv()
        started += lasts[third]
        total = f3[third, mine] + r3[third, 0] + r3[third, 1] + r3[third, 2]
        for channel in range(OWN):
            lanes = pl.ds(channel * TAPS + third * THIRD, THIRD)
            row[0:1, lanes] = total[channel : channel + 1]

    share = project(salt, owner * RUN, row, grow, bits, acc)

    share = share * (1.0 / math.sqrt(9.0 * CH * CH))
    me = at["x"] * 2 + at["core"]
    sum8[me] = share
    group = []
    for index, peer in enumerate(peers[:7]):
        group.append(send(sum8.at[me], sum8.at[me], all_send.at[index], all_recv.at[index], peer))
    for copy in group:
        copy.wait_recv()
    started += group
    share = sum8[0]
    for index in range(1, 8):
        share = share + sum8[index]
    for axis, slots, base in (("y", sum4, 7), ("z", sum4b, 10)):
        me = at[axis]
        slots[me] = share
        group = []
        for index in range(3):
            group.append(send(slots.at[me], slots.at[me], all_send.at[base + index],
                              all_recv.at[base + index], peers[base + index]))
        for copy in group:
            copy.wait_recv()
        started += group
        share = slots[0] + slots[1] + slots[2] + slots[3]
    out_ref[...] = share
    for copy in started:
        copy.wait_send()


def back(salt, cot, hid):
    bf16, full = jnp.bfloat16, jnp.float32
    vmem = pltpu.VMEM
    dma = pltpu.SemaphoreType.DMA
    return pl.pallas_call(
        back_kernel,
        out_shape=jax.ShapeDtypeStruct((1, K), full),
        in_specs=[
            pl.BlockSpec(memory_space=pltpu.SMEM),
            pl.BlockSpec(memory_space=pltpu.VMEM),
            pl.BlockSpec(memory_space=pltpu.VMEM),
        ],
        out_specs=pl.BlockSpec(memory_space=pltpu.VMEM),
        scratch_shapes=[
            vmem((256, CH), bf16),
            vmem((3, 10, 32, CH), bf16),
            vmem((3, 2, 320, 256), bf16),
            vmem((3, 4, 80, THIRD), bf16),
            vmem((3, 80, CUT), bf16),
            vmem((3, 80, THIRD - CUT), bf16),
            vmem((3, 2, 80, THIRD), bf16),
            vmem((3, 4, 24, THIRD), full),
            vmem((3, 4, 32, THIRD), bf16),
            vmem((3, 32, CUT), bf16),
            vmem((3, 32, THIRD - CUT), bf16),
            vmem((3, 2, 32, THIRD), bf16),
            vmem((3, 4, 8, THIRD), full),
            vmem((3, 3, 8, THIRD), full),
            vmem((1, PADDED), full),
            vmem((32, PADDED), F8),
            vmem((32, K), full),
            vmem((PADDED, K), F8),
            vmem((8, 1, K), full),
            vmem((4, 1, K), full),
            vmem((4, 1, K), full),
            dma((2,)), dma((2,)),
            dma((3, 2, 4)), dma((3, 2, 4)),
            dma((3, 3)), dma((3, 3)),
            dma((13,)), dma((13,)),
        ],
        compiler_params=pltpu.CompilerParams(
            collective_id=0, has_side_effects=True, vmem_limit_bytes=60 * 2**20
        ),
    )(salt, cot, hid)


def unfold(padded, tile_rows, tile_cols):
    pieces = []
    for row_off in range(3):
        for col_off in range(3):
            pieces.append(
                padded[:, row_off : row_off + tile_rows, col_off : col_off + tile_cols, :]
            )
    joined = jnp.concatenate(pieces, axis=3)
    return joined.reshape(joined.shape[0], tile_rows * tile_cols, joined.shape[3])


def on_device(
    latent, timestep, noise_seed, proj_seed, example_ids, time_weight, conv1_weight, conv2_weight
):
    batch, tile_rows, tile_cols, channels = latent.shape
    rows_count = lax.axis_size("row")
    cols_count = lax.axis_size("col")
    rows_all = tile_rows * rows_count
    cols_all = tile_cols * cols_count
    row_first = lax.axis_index("row") * tile_rows
    col_first = lax.axis_index("col") * tile_cols
    noise = noise_field(
        example_ids, noise_seed, row_first, col_first, tile_rows, tile_cols, channels, rows_all, cols_all
    )
    abar = plan(timestep)[:, None, None, None]
    noisy = (jnp.sqrt(abar) * latent.astype(jnp.float32) + jnp.sqrt(1.0 - abar) * noise).astype(
        jnp.bfloat16
    )
    act = jax.nn.silu(noisy.astype(jnp.float32)).astype(jnp.bfloat16)
    act_pad = extended(act, (("row", 1), ("col", 2)), 1)
    features = time_features(timestep, channels).astype(jnp.bfloat16)
    temb = jnp.dot(features, time_weight, preferred_element_type=jnp.float32)
    act_cols = unfold(act_pad, tile_rows, tile_cols).reshape(
        batch * tile_rows * tile_cols, 9 * channels
    )
    pre = jnp.dot(act_cols, conv1_weight, preferred_element_type=jnp.float32).reshape(
        batch, tile_rows, tile_cols, channels
    )
    hidden = jax.nn.silu(pre + temb[:, None, None, :]).astype(jnp.bfloat16)
    hid_pad = extended(hidden, (("row", 1), ("col", 2)), 1)
    hid_cols = unfold(hid_pad, tile_rows, tile_cols)
    conv_out = jnp.dot(
        hid_cols.reshape(batch * tile_rows * tile_cols, 9 * channels),
        conv2_weight,
        preferred_element_type=jnp.float32,
    )
    out_full = noisy.astype(jnp.float32) + conv_out.reshape(batch, tile_rows, tile_cols, channels)
    section_out = out_full.astype(jnp.bfloat16)
    cot = ((out_full - noise) / math.sqrt(rows_all * cols_all)).astype(jnp.bfloat16)
    cot = cot.reshape(batch * tile_rows * tile_cols, channels)
    shifted = jnp.stack([hid_pad[0, :, dx : dx + tile_cols, :] for dx in range(3)])
    salt = mix_bits(proj_seed + jnp.int32(12345))
    sketch = back(salt, cot, shifted)
    return (section_out, sketch)


def solution(mesh):
    placed = (P(None, "row", "col", None), P(), P(), P(), P(), P(), P(), P())
    return jax.shard_map(
        on_device,
        mesh=mesh,
        in_specs=placed,
        out_specs=(P(None, "row", "col", None), P()),
        check_vma=False,
    )
```

```python
import functools
import math

import jax
import jax.numpy as jnp
from jax import lax
from jax.experimental import pallas as pl
from jax.experimental.pallas import tpu as pltpu
from jax.sharding import PartitionSpec as P

K = 1024
FILLS = (12, 12, 4, 8, 24, 8, 14)
M1 = 2146121005
M2 = -2073254261
MESH = pl.DeviceIdType.MESH


def wrap32(value):
    value &= 0xFFFFFFFF
    return value - (1 << 32) if value >= (1 << 31) else value


def mix_bits(value):
    value = value ^ lax.shift_right_logical(value, jnp.int32(16))
    value = value * jnp.int32(M1)
    value = value ^ lax.shift_right_logical(value, jnp.int32(15))
    value = value * jnp.int32(M2)
    value = value ^ lax.shift_right_logical(value, jnp.int32(16))
    return value


CH = 640
ROWS = 128
COLS = 256
TH = 8
TW = 32
TAPS = 9 * CH
THIRD = 3 * CH
CUT = 1024
OWN = 5
RUN = OWN * TAPS
PADDED = 29184
BLOCK = 4864
F8 = jnp.float8_e4m3fn
PARTS = 4
ORDERS = (("x", "y", "z"), ("y", "z", "x"), ("z", "x", "y"))


def place():
    r = lax.axis_index("row")
    c = lax.axis_index("col")
    return {
        "core": lax.rem(r, 2),
        "x": lax.rem(r // 2, 4),
        "y": lax.rem(c, 2) * 2 + r // 8,
        "z": c // 2,
    }


def device(at, **moved):
    at = {**at, **moved}
    row = (lax.rem(at["y"], 2) * 4 + at["x"]) * 2 + at["core"]
    return (row, at["z"] * 2 + at["y"] // 2)


def hop(at, axis, by):
    return lax.rem(at[axis] + (by + 4), 4)


def peers_of(at):
    out = []
    for step in range(4):
        for flip in range(2):
            if step or flip:
                out.append(device(at, x=hop(at, "x", step), core=lax.rem(at["core"] + flip, 2)))
    for axis in ("y", "z"):
        for step in range(1, 4):
            out.append(device(at, **{axis: hop(at, axis, step)}))
    return out


def silu(value):
    return value / (1.0 + jnp.exp(-value))


def rounded(value):
    return value.astype(jnp.bfloat16)


def field(rows, cols, example, salt):
    lane = lax.broadcasted_iota(jnp.int32, (1, CH), 1)
    base = ((example * ROWS + rows) * COLS + cols) * (4 * CH) + salt
    base = base + lane * 4
    total = None
    for index in range(4):
        bits = shift_right(mix_bits(base + index), 8)
        total = bits if total is None else total + bits
    return (f32(total) * (1.0 / 16777216.0) - 2.0) * math.sqrt(3.0)


def inside(rows, cols):
    return (rows >= 0) & (rows < ROWS) & (cols >= 0) & (cols < COLS)


def selection(third, core):
    row = lax.broadcasted_iota(jnp.int32, (320, 1), 0)
    owner = lax.shift_right_logical(row * 52429, jnp.int32(18))
    channel = row - owner * OWN
    digits = (lax.shift_right_logical(owner, jnp.int32(4)), lax.shift_right_logical(owner, jnp.int32(2)) & 3, owner & 3)
    named = dict(zip(ORDERS[third], digits))
    wanted = ((core * 4 + named["x"]) * 4 + named["y"]) * 4 + named["z"]
    wanted = wanted * OWN + channel
    lane = lax.broadcasted_iota(jnp.int32, (320, CH), 1)
    return jnp.where(lane == wanted, 1.0, 0.0).astype(jnp.bfloat16)


def f32(value):
    return value.astype(jnp.float32)


def shift_right(value, by):
    return lax.shift_right_logical(value, jnp.int32(by))


def alignment(salt, first):
    m_first = (first + shift_right(salt, 10)) & jnp.int32((1 << 22) - 1)
    ahead = m_first & 255
    return ahead, shift_right(m_first - ahead, 6)


def make_signs(salt, first, bits, low, high):
    h_first = alignment(salt, first)[1]
    lane = lax.broadcasted_iota(jnp.int32, (1, 128), 1)
    m_row = lax.broadcasted_iota(jnp.int32, (32, 128), 0)

    def body(step, carry):
        h_four = (h_first + step * 4) & 65535
        high_bits = shift_right(h_four, 10)
        columns = [((m_row + half) ^ high_bits) * jnp.int32(wrap32(1024 * M1)) for half in (0, 32)]
        for part in range(4):
            h = h_four + part
            for j in range(0, K, 128):
                line = ((lane + j) ^ (h & 1023)) * jnp.int32(M1) + h * jnp.int32(wrap32(65536 * M1))
                line = jnp.broadcast_to(line, (32, 128))
                for half in range(2):
                    w = line + columns[half]
                    y = (w ^ shift_right(w, 15)) * jnp.int32(M2)
                    rows = pl.ds(pl.multiple_of(step * 256 + part * 64 + half * 32, 32), 32)
                    bits[rows, j : j + 128] = lax.shift_right_arithmetic(y, 31).astype(jnp.int8).astype(F8)
        return carry

    lax.fori_loop(low, high, body, 0)


def project(salt, first, row, grow, bits, acc):
    s = salt & (K - 1)
    ahead = alignment(salt, first)[0]
    flat = row[...]
    whole = jnp.sum(flat)
    largest = jnp.maximum(jnp.max(jnp.abs(flat)), 1e-30)
    one = pltpu.roll(flat * (16.0 / largest), ahead, axis=1)
    two = pltpu.roll(one, 1, axis=1)
    for block in range(PADDED // BLOCK):
        lanes = slice(block * BLOCK, (block + 1) * BLOCK)
        pair = jnp.concatenate([one[:, lanes], two[:, lanes]], axis=0)
        pieces = []
        for _ in range(PARTS):
            piece = lax.round(pair, lax.RoundingMethod.TO_NEAREST_EVEN)
            pieces.append(piece)
            pair = (pair - piece) * 32.0
        pieces.append(jnp.zeros((24, BLOCK), jnp.float32))
        grow[:, lanes] = jnp.concatenate(pieces, axis=0).astype(F8)
    acc[...] = jnp.zeros_like(acc)

    def body(step, carry):
        lanes = pl.ds(pl.multiple_of(step * BLOCK, BLOCK), BLOCK)
        acc[...] += jnp.dot(grow[:, lanes], bits[lanes, :], preferred_element_type=jnp.float32)
        return carry

    lax.fori_loop(0, PADDED // BLOCK, body, 0)
    total = acc[6:8, :]
    for index in (2, 1, 0):
        total = acc[2 * index : 2 * index + 2, :] + total * (1.0 / 32.0)
    total = whole + total * (largest * (2.0 / 16.0))
    j = lax.broadcasted_iota(jnp.int32, (1, K), 1)
    return pltpu.roll(jnp.where(j >= s, total[0:1], total[1:2]), (K - s) & (K - 1), axis=1)


def kernel(
    step_ref, noise_seed_ref, proj_seed_ref, example_ref, latent_ref, time_ref, w1_ref, w2_ref,
    section_ref, out_ref,
    stage, tall, side_in, corner_in, weight, actx, side_lhs, noise_keep, noisy_keep,
    hid_near, hid_far, cot_near, cot_far,
    lhs, s1, r1a, r1b, r1, s2, r2a, r2b, r2, f3, r3, row, grow, acc, bits,
    sum8, sum4, sum4b,
    load_sem, rim_send, rim_recv,
    pair_send, pair_recv, ring_send, ring_recv, tail_send, tail_recv, all_send, all_recv,
):
    at = place()
    r_index = lax.axis_index("row")
    c_index = lax.axis_index("col")
    peers = peers_of(at)
    around = []
    for dr in (-1, 0, 1):
        for dc in (-1, 0, 1):
            if dr or dc:
                around.append((dr, dc))

    def beside(dr, dc):
        return (lax.rem(r_index + (16 + dr), 16), lax.rem(c_index + (8 + dc), 8))

    barrier = pltpu.get_barrier_semaphore()
    greeted = peers + [beside(dr, dc) for dr, dc in around]
    for peer in greeted:
        pl.semaphore_signal(barrier, inc=1, device_id=peer, device_id_type=MESH)

    def load(source, part):
        rows = pl.ds(part * THIRD, THIRD)
        return pltpu.make_async_copy(source.at[rows], weight.at[rows], load_sem.at[part])

    for part in range(3):
        load(w1_ref, part).start()

    salt = mix_bits(proj_seed_ref[0] + jnp.int32(12345))
    owner = ((at["core"] * 4 + at["x"]) * 4 + at["y"]) * 4 + at["z"]
    marks = [0]

    def fill(count):
        low = marks[-1]
        high = min(low + count, PADDED // 256)
        marks.append(high)
        if high > low:
            make_signs(salt, owner * RUN, bits, low, high)

    def pack(cells):
        rows = [f32(latent_ref[0, r])[c : c + 1] for r, c in cells]
        if len(rows) < 16:
            rows.append(jnp.zeros((16 - len(rows), CH), jnp.float32))
        return rounded(jnp.concatenate(rows, axis=0))

    edge = {-1: (0, 1), 1: (TW - 2, TW - 1)}
    brim = {-1: (0, 1), 1: (TH - 2, TH - 1)}
    for index, dc in enumerate((-1, 1)):
        stage[index] = pack([(r, c) for c in edge[dc] for r in range(TH)])
        for other, dr in enumerate((-1, 1)):
            stage[2 + other * 2 + index] = pack([(r, c) for c in edge[dc] for r in brim[dr]])

    example = example_ref[0]
    noise_salt = mix_bits(noise_seed_ref[0])
    row_first = r_index * TH
    col_first = c_index * TW
    when = jnp.broadcast_to(step_ref[0], (1, CH)).astype(jnp.float32)
    abar = jnp.cos((when / 1000.0 + 0.008) / 1.008 * (math.pi / 2.0)) ** 2
    keep = jnp.sqrt(abar)
    spoil = jnp.sqrt(1.0 - abar)
    col_here = lax.broadcasted_iota(jnp.int32, (TW, 1), 0)

    def noised(latent, rows, cols):
        noise = field(rows, cols, example, noise_salt)
        noisy = rounded(keep * f32(latent) + spoil * noise)
        act = f32(rounded(silu(f32(noisy))))
        return noise, noisy, act

    def middle(r):
        latent = latent_ref[0, r]
        noise, noisy, act = noised(latent, col_here * 0 + (row_first + r), col_first + col_here)
        noise_keep[r] = noise
        noisy_keep[r] = noisy
        actx[r + 2, :, CH : 2 * CH] = rounded(act)

    def middles(r, carry):
        middle(r)
        return carry

    lax.fori_loop(0, TH, middles, 0)
    fill(FILLS[0])
    pl.semaphore_wait(barrier, len(greeted))

    def send(src, dst, send_sem, recv_sem, to):
        copy = pltpu.make_async_remote_copy(
            src_ref=src, dst_ref=dst, send_sem=send_sem, recv_sem=recv_sem,
            device_id=to, device_id_type=MESH,
        )
        copy.start()
        return copy

    rims = []
    for index, (dr, dc) in enumerate(around):
        if dc == 0:
            src = latent_ref.at[0, pl.ds(brim[dr][0], 2)]
            dst = tall.at[0 if dr > 0 else 1]
        elif dr == 0:
            src = stage.at[0 if dc < 0 else 1]
            dst = side_in.at[0 if dc > 0 else 1]
        else:
            src = stage.at[2 + (0 if dr < 0 else 2) + (0 if dc < 0 else 1)]
            dst = corner_in.at[(0 if dr > 0 else 2) + (0 if dc > 0 else 1)]
        rims.append(send(src, dst, rim_send.at[index], rim_recv.at[index], beside(dr, dc)))
    started = list(rims)

    lane = lax.broadcasted_iota(jnp.int32, (1, CH), 1)
    half = jnp.where(lane < CH // 2, lane, lane - CH // 2)
    angle = when * jnp.exp(f32(half) * (-math.log(10000.0)) / (CH // 2))
    wave = jnp.where(lane < CH // 2, jnp.sin(angle), jnp.cos(angle))
    wave = rounded(jnp.concatenate([wave, jnp.zeros((15, CH), jnp.float32)], axis=0))
    temb = jnp.dot(wave, time_ref[...], preferred_element_type=jnp.float32)[0:1]
    fill(FILLS[1])
    for copy in rims:
        copy.wait_recv()

    def outer(which, r, grid_row):
        rows = col_here * 0 + grid_row
        cols = col_first + col_here
        act = noised(tall[which, r], rows, cols)[2]
        return jnp.where(inside(rows, cols), act, 0.0)

    for which, first in ((0, -2), (1, TH)):
        for r in range(2):
            act = outer(which, r, row_first + (first + r))
            actx[first + 2 + r, :, CH : 2 * CH] = rounded(act)
    flank = lax.broadcasted_iota(jnp.int32, (16, 1), 0)
    sides = []
    for index, first in enumerate((-2, TW)):
        rows = row_first + (flank & 7)
        cols = col_first + first + shift_right(flank, 3)
        act = noised(side_in[index], rows, cols)[2]
        sides.append(jnp.where(inside(rows, cols), act, 0.0))
    corners = jnp.concatenate([f32(corner_in[index])[0:4] for index in range(4)], axis=0)
    kind = shift_right(flank, 2)
    rows = row_first + (flank & 1) + jnp.where(kind < 2, -2, TH)
    cols = col_first + (shift_right(flank, 1) & 1) + jnp.where((kind & 1) == 0, -2, TW)
    corners = jnp.where(inside(rows, cols), noised(corners, rows, cols)[2], 0.0)

    def column(side, which):
        top = corners[4 * side + 2 * which : 4 * side + 2 * which + 2]
        bottom = corners[8 + 4 * side + 2 * which : 8 + 4 * side + 2 * which + 2]
        return jnp.concatenate([top, sides[side][8 * which : 8 * which + 8], bottom], axis=0)

    centre = [f32(actx[r, :, CH : 2 * CH]) for r in range(TH + 4)]
    lefts = [column(0, 0), column(0, 1), jnp.concatenate([c[0:1] for c in centre], axis=0)]
    rights = [jnp.concatenate([c[TW - 1 : TW] for c in centre], axis=0), column(1, 0), column(1, 1)]
    for r in range(TH + 4):
        cell = centre[r]
        actx[r, :, 0:CH] = rounded(
            jnp.where(col_here == 0, lefts[1][r : r + 1], pltpu.roll(cell, 1, axis=0))
        )
        actx[r, :, 2 * CH : 3 * CH] = rounded(
            jnp.where(col_here == TW - 1, rights[1][r : r + 1], pltpu.roll(cell, TW - 1, axis=0))
        )
    for dy in range(3):
        for dx in range(3):
            both = [lefts[dx][dy : dy + 10], rights[dx][dy : dy + 10], jnp.zeros((12, CH), jnp.float32)]
            side_lhs[dy, :, dx * CH : (dx + 1) * CH] = rounded(jnp.concatenate(both, axis=0))

    total = None
    for dy in range(3):
        load(w1_ref, dy).wait()
        left = jnp.concatenate(
            [actx[dy : dy + TH + 2].reshape((TH + 2) * TW, THIRD), side_lhs[dy]], axis=0
        )
        part = jnp.dot(left, weight[dy * THIRD : (dy + 1) * THIRD], preferred_element_type=jnp.float32)
        total = part if total is None else total + part
        load(w2_ref, dy).start()
    hidden = silu(total + temb)
    flanks = hidden[(TH + 2) * TW :]
    flank = lax.broadcasted_iota(jnp.int32, (32, 1), 0)
    right_side = jnp.where(flank < 10, 0, 1)
    rows = row_first - 1 + flank - right_side * 10
    cols = col_first - 1 + right_side * (TW + 1)
    flanks = jnp.where(inside(rows, cols), flanks, 0.0)
    for r in range(TH + 2):
        cell = hidden[r * TW : (r + 1) * TW]
        if r in (0, TH + 1):
            rows = col_here * 0 + (row_first + (r - 1))
            cell = jnp.where(inside(rows, col_first + col_here), cell, 0.0)
        hid_near[r, :, CH : 2 * CH] = rounded(cell)
        hid_near[r, :, 0:CH] = rounded(
            jnp.where(col_here == 0, flanks[r : r + 1], pltpu.roll(cell, 1, axis=0))
        )
        hid_near[r, :, 2 * CH : 3 * CH] = rounded(
            jnp.where(col_here == TW - 1, flanks[10 + r : 11 + r], pltpu.roll(cell, TW - 1, axis=0))
        )

    partner = device(at, core=lax.rem(at["core"] + 1, 2))
    pair = [send(hid_near, hid_far, pair_send.at[1], pair_recv.at[1], partner)]
    fill(FILLS[2])

    total = None
    for dy in range(3):
        load(w2_ref, dy).wait()
        part = jnp.dot(
            hid_near[dy : dy + TH].reshape(TH * TW, THIRD), weight[dy * THIRD : (dy + 1) * THIRD],
            preferred_element_type=jnp.float32,
        )
        total = part if total is None else total + part
    for r in range(TH):
        full = f32(noisy_keep[r]) + total[r * TW : (r + 1) * TW]
        section_ref[0, r] = rounded(full)
        cot_near[r * TW : (r + 1) * TW] = rounded((full - noise_keep[r]) * (1.0 / math.sqrt(ROWS * COLS)))
    pair.append(send(cot_near, cot_far, pair_send.at[0], pair_recv.at[0], partner))
    started += pair
    picks = [selection(third, at["core"]) for third in range(3)]

    def gather(side, cot):
        for third in range(3):
            lhs[third, side] = lax.dot_general(
                picks[third], cot[...], (((1,), (1,)), ((), ())), preferred_element_type=jnp.float32
            ).astype(jnp.bfloat16)

    gather(0, cot_near)
    for copy in pair:
        copy.wait_recv()
    gather(1, cot_far)

    def ring_one(third, level, blocks, ra, rb):
        axis = ORDERS[third][level]
        mine = at[axis]
        up = device(at, **{axis: hop(at, axis, 1)})
        down = device(at, **{axis: hop(at, axis, -1)})
        across = hop(at, axis, 2)
        sems = (third, level)
        return [
            send(blocks.at[third, across, :, pl.ds(0, CUT)], ra.at[third],
                 ring_send.at[third, level, 0], ring_recv.at[third, level, 0], up),
            send(blocks.at[third, across, :, pl.ds(CUT, THIRD - CUT)], rb.at[third],
                 ring_send.at[third, level, 1], ring_recv.at[third, level, 1], down),
        ]

    def ring_two(third, level, blocks, ra, rb, first, landed):
        axis = ORDERS[third][level]
        above = hop(at, axis, 1)
        below = hop(at, axis, -1)
        first[0].wait_recv()
        old = blocks[third, above, :, 0:CUT]
        blocks[third, above, :, 0:CUT] = (f32(old) + f32(ra[third])).astype(jnp.bfloat16)
        up = send(blocks.at[third, above], landed.at[third, 0],
                  ring_send.at[third, level, 2], ring_recv.at[third, level, 2],
                  device(at, **{axis: above}))
        first[1].wait_recv()
        old = blocks[third, below, :, CUT:THIRD]
        blocks[third, below, :, CUT:THIRD] = (f32(old) + f32(rb[third])).astype(jnp.bfloat16)
        down = send(blocks.at[third, below], landed.at[third, 1],
                    ring_send.at[third, level, 3], ring_recv.at[third, level, 3],
                    device(at, **{axis: below}))
        return [up, down]

    ones = []
    for third in range(3):
        near = hid_near[third : third + TH].reshape(TH * TW, THIRD)
        far = hid_far[third : third + TH].reshape(TH * TW, THIRD)
        total = jnp.dot(lhs[third, 0], near, preferred_element_type=jnp.float32)
        total += jnp.dot(lhs[third, 1], far, preferred_element_type=jnp.float32)
        s1[third] = rounded(total).reshape(4, 80, THIRD)
        ones.append(ring_one(third, 0, s1, r1a, r1b))
    fill(FILLS[3])
    twos = [ring_two(t, 0, s1, r1a, r1b, ones[t], r1) for t in range(3)]
    started += [copy for group in ones + twos for copy in group]
    fill(FILLS[4])
    ones = []
    for third in range(3):
        mine = at[ORDERS[third][0]]
        for copy in twos[third]:
            copy.wait_recv()
        total = f32(s1[third, mine]) + f32(r1[third, 0]) + f32(r1[third, 1])
        for block in range(4):
            piece = total[block * 20 : block * 20 + 20]
            s2[third, block] = jnp.concatenate([piece, jnp.zeros((12, THIRD), jnp.float32)], axis=0).astype(
                jnp.bfloat16
            )
        ones.append(ring_one(third, 1, s2, r2a, r2b))
    fill(FILLS[5])
    twos = [ring_two(t, 1, s2, r2a, r2b, ones[t], r2) for t in range(3)]
    started += [copy for group in ones + twos for copy in group]
    fill(FILLS[6])
    lasts = []
    for third in range(3):
        mine = at[ORDERS[third][1]]
        for copy in twos[third]:
            copy.wait_recv()
        total = f32(s2[third, mine, 0:20]) + f32(r2[third, 0, 0:20]) + f32(r2[third, 1, 0:20])
        for block in range(4):
            f3[third, block] = jnp.concatenate(
                [total[block * OWN : (block + 1) * OWN], jnp.zeros((3, THIRD), jnp.float32)], axis=0
            )
        axis = ORDERS[third][2]
        group = []
        for step in range(1, 4):
            to = hop(at, axis, step)
            group.append(
                send(f3.at[third, to], r3.at[third, step - 1],
                     tail_send.at[third, step - 1], tail_recv.at[third, step - 1],
                     device(at, **{axis: to}))
            )
        lasts.append(group)
    fill(PADDED)
    row[...] = jnp.zeros_like(row)
    for third in range(3):
        mine = at[ORDERS[third][2]]
        for copy in lasts[third]:
            copy.wait_recv()
        started += lasts[third]
        total = f3[third, mine] + r3[third, 0] + r3[third, 1] + r3[third, 2]
        for channel in range(OWN):
            lanes = pl.ds(channel * TAPS + third * THIRD, THIRD)
            row[0:1, lanes] = total[channel : channel + 1]

    share = project(salt, owner * RUN, row, grow, bits, acc)

    share = share * (1.0 / math.sqrt(9.0 * CH * CH))
    me = at["x"] * 2 + at["core"]
    sum8[me] = share
    group = []
    for index, peer in enumerate(peers[:7]):
        group.append(send(sum8.at[me], sum8.at[me], all_send.at[index], all_recv.at[index], peer))
    for copy in group:
        copy.wait_recv()
    started += group
    share = sum8[0]
    for index in range(1, 8):
        share = share + sum8[index]
    for axis, slots, base in (("y", sum4, 7), ("z", sum4b, 10)):
        me = at[axis]
        slots[me] = share
        group = []
        for index in range(3):
            group.append(send(slots.at[me], slots.at[me], all_send.at[base + index],
                              all_recv.at[base + index], peers[base + index]))
        for copy in group:
            copy.wait_recv()
        started += group
        share = slots[0] + slots[1] + slots[2] + slots[3]
    out_ref[...] = share
    for copy in started:
        copy.wait_send()


def call(step, noise_seed, proj_seed, example, latent, time_weight, w1, w2):
    bf16, full = jnp.bfloat16, jnp.float32
    vmem = pltpu.VMEM
    dma = pltpu.SemaphoreType.DMA
    scalar = pl.BlockSpec(memory_space=pltpu.SMEM)
    near = pl.BlockSpec(memory_space=pltpu.VMEM)
    return pl.pallas_call(
        kernel,
        out_shape=(
            jax.ShapeDtypeStruct(latent.shape, bf16),
            jax.ShapeDtypeStruct((1, K), full),
        ),
        in_specs=[scalar] * 4 + [near] * 2 + [pl.BlockSpec(memory_space=pl.ANY)] * 2,
        out_specs=(near, near),
        scratch_shapes=[
            vmem((6, 16, CH), bf16),
            vmem((2, 2, TW, CH), bf16),
            vmem((2, 16, CH), bf16),
            vmem((4, 16, CH), bf16),
            vmem((TAPS, CH), bf16),
            vmem((TH + 4, TW, THIRD), bf16),
            vmem((3, 32, THIRD), bf16),
            vmem((TH, TW, CH), full),
            vmem((TH, TW, CH), bf16),
            vmem((TH + 2, TW, THIRD), bf16),
            vmem((TH + 2, TW, THIRD), bf16),
            vmem((TH * TW, CH), bf16),
            vmem((TH * TW, CH), bf16),
            vmem((3, 2, 320, 256), bf16),
            vmem((3, 4, 80, THIRD), bf16),
            vmem((3, 80, CUT), bf16),
            vmem((3, 80, THIRD - CUT), bf16),
            vmem((3, 2, 80, THIRD), bf16),
            vmem((3, 4, 32, THIRD), bf16),
            vmem((3, 32, CUT), bf16),
            vmem((3, 32, THIRD - CUT), bf16),
            vmem((3, 2, 32, THIRD), bf16),
            vmem((3, 4, 8, THIRD), full),
            vmem((3, 3, 8, THIRD), full),
            vmem((1, PADDED), full),
            vmem((32, PADDED), F8),
            vmem((32, K), full),
            vmem((PADDED, K), F8),
            vmem((8, 1, K), full),
            vmem((4, 1, K), full),
            vmem((4, 1, K), full),
            dma((3,)),
            dma((8,)), dma((8,)),
            dma((2,)), dma((2,)),
            dma((3, 2, 4)), dma((3, 2, 4)),
            dma((3, 3)), dma((3, 3)),
            dma((13,)), dma((13,)),
        ],
        compiler_params=pltpu.CompilerParams(
            collective_id=0, has_side_effects=True, vmem_limit_bytes=60 * 2**20
        ),
    )(step, noise_seed, proj_seed, example, latent, time_weight, w1, w2)


def on_device(
    latent, timestep, noise_seed, proj_seed, example_ids, time_weight, conv1_weight, conv2_weight
):
    return call(
        timestep, noise_seed, proj_seed, example_ids, latent, time_weight, conv1_weight, conv2_weight
    )


def solution(mesh):
    placed = (P(None, "row", "col", None), P(), P(), P(), P(), P(), P(), P())
    return jax.shard_map(
        on_device,
        mesh=mesh,
        in_specs=placed,
        out_specs=(P(None, "row", "col", None), P()),
        check_vma=False,
    )
```

```python
import functools
import math

import jax
import jax.numpy as jnp
from jax import lax
from jax.experimental import pallas as pl
from jax.experimental.pallas import tpu as pltpu
from jax.sharding import PartitionSpec as P

K = 1024
FILLS = (8, 8, 0, 18, 34, 26)
M1 = 2146121005
M2 = -2073254261
MESH = pl.DeviceIdType.MESH


def wrap32(value):
    value &= 0xFFFFFFFF
    return value - (1 << 32) if value >= (1 << 31) else value


def mix_bits(value):
    value = value ^ lax.shift_right_logical(value, jnp.int32(16))
    value = value * jnp.int32(M1)
    value = value ^ lax.shift_right_logical(value, jnp.int32(15))
    value = value * jnp.int32(M2)
    value = value ^ lax.shift_right_logical(value, jnp.int32(16))
    return value


CH = 640
ROWS = 128
COLS = 256
TH = 8
TW = 32
TAPS = 9 * CH
THIRD = 3 * CH
TILES = THIRD // 128
CUT = 1024
OWN = 5
RUN = OWN * TAPS
PADDED = 29184
BLOCK = 4864
F8 = jnp.float8_e4m3fn
PARTS = 4
ORDERS = (("x", "y", "z"), ("y", "z", "x"), ("z", "x", "y"))


def place():
    r = lax.axis_index("row")
    c = lax.axis_index("col")
    return {
        "core": lax.rem(r, 2),
        "x": lax.rem(r // 2, 4),
        "y": lax.rem(c, 2) * 2 + r // 8,
        "z": c // 2,
    }


def device(at, **moved):
    at = {**at, **moved}
    row = (lax.rem(at["y"], 2) * 4 + at["x"]) * 2 + at["core"]
    return (row, at["z"] * 2 + at["y"] // 2)


def hop(at, axis, by):
    return lax.rem(at[axis] + (by + 4), 4)


def peers_of(at):
    out = []
    for step in range(4):
        for flip in range(2):
            if step or flip:
                out.append(device(at, x=hop(at, "x", step), core=lax.rem(at["core"] + flip, 2)))
    for up in range(4):
        for deep in range(4):
            if up or deep:
                out.append(device(at, y=hop(at, "y", up), z=hop(at, "z", deep)))
    return out


def silu(value):
    return value / (1.0 + jnp.exp(-value))


def rounded(value):
    return value.astype(jnp.bfloat16)


def field(rows, cols, example, salt):
    lane = lax.broadcasted_iota(jnp.int32, (1, CH), 1)
    base = ((example * ROWS + rows) * COLS + cols) * (4 * CH) + salt
    base = base + lane * 4
    total = None
    for index in range(4):
        bits = shift_right(mix_bits(base + index), 8)
        total = bits if total is None else total + bits
    return (f32(total) * (1.0 / 16777216.0) - 2.0) * math.sqrt(3.0)


def inside(rows, cols):
    return (rows >= 0) & (rows < ROWS) & (cols >= 0) & (cols < COLS)


def selection(third, core):
    row = lax.broadcasted_iota(jnp.int32, (320, 1), 0)
    owner = lax.shift_right_logical(row * 52429, jnp.int32(18))
    channel = row - owner * OWN
    digits = (lax.shift_right_logical(owner, jnp.int32(4)), lax.shift_right_logical(owner, jnp.int32(2)) & 3, owner & 3)
    named = dict(zip(ORDERS[third], digits))
    wanted = ((core * 4 + named["x"]) * 4 + named["y"]) * 4 + named["z"]
    wanted = wanted * OWN + channel
    lane = lax.broadcasted_iota(jnp.int32, (320, CH), 1)
    return jnp.where(lane == wanted, 1.0, 0.0).astype(jnp.bfloat16)


def f32(value):
    return value.astype(jnp.float32)


def shift_right(value, by):
    return lax.shift_right_logical(value, jnp.int32(by))


def alignment(salt, first):
    m_first = (first + shift_right(salt, 10)) & jnp.int32((1 << 22) - 1)
    ahead = m_first & 255
    return ahead, shift_right(m_first - ahead, 6)


def make_signs(salt, first, bits, low, high):
    h_first = alignment(salt, first)[1]
    lane = lax.broadcasted_iota(jnp.int32, (1, 128), 1)
    m_row = lax.broadcasted_iota(jnp.int32, (32, 128), 0)

    def body(step, carry):
        h_four = (h_first + step * 4) & 65535
        high_bits = shift_right(h_four, 10)
        columns = [((m_row + half) ^ high_bits) * jnp.int32(wrap32(1024 * M1)) for half in (0, 32)]
        for part in range(4):
            h = h_four + part
            for j in range(0, K, 128):
                line = ((lane + j) ^ (h & 1023)) * jnp.int32(M1) + h * jnp.int32(wrap32(65536 * M1))
                line = jnp.broadcast_to(line, (32, 128))
                for half in range(2):
                    w = line + columns[half]
                    y = (w ^ shift_right(w, 15)) * jnp.int32(M2)
                    rows = pl.ds(pl.multiple_of(step * 256 + part * 64 + half * 32, 32), 32)
                    bits[rows, j : j + 128] = lax.shift_right_arithmetic(y, 31).astype(jnp.int8).astype(F8)
        return carry

    lax.fori_loop(low, high, body, 0)


def project(salt, first, row, grow, bits, acc):
    s = salt & (K - 1)
    ahead = alignment(salt, first)[0]
    flat = row[...]
    whole = jnp.sum(flat)
    largest = jnp.maximum(jnp.max(jnp.abs(flat)), 1e-30)
    one = pltpu.roll(flat * (16.0 / largest), ahead, axis=1)
    two = pltpu.roll(one, 1, axis=1)
    for block in range(PADDED // BLOCK):
        lanes = slice(block * BLOCK, (block + 1) * BLOCK)
        pair = jnp.concatenate([one[:, lanes], two[:, lanes]], axis=0)
        pieces = []
        for _ in range(PARTS):
            piece = lax.round(pair, lax.RoundingMethod.TO_NEAREST_EVEN)
            pieces.append(piece)
            pair = (pair - piece) * 32.0
        pieces.append(jnp.zeros((24, BLOCK), jnp.float32))
        grow[:, lanes] = jnp.concatenate(pieces, axis=0).astype(F8)
    acc[...] = jnp.zeros_like(acc)

    def body(step, carry):
        lanes = pl.ds(pl.multiple_of(step * BLOCK, BLOCK), BLOCK)
        acc[...] += jnp.dot(grow[:, lanes], bits[lanes, :], preferred_element_type=jnp.float32)
        return carry

    lax.fori_loop(0, PADDED // BLOCK, body, 0)
    total = acc[6:8, :]
    for index in (2, 1, 0):
        total = acc[2 * index : 2 * index + 2, :] + total * (1.0 / 32.0)
    total = whole + total * (largest * (2.0 / 16.0))
    j = lax.broadcasted_iota(jnp.int32, (1, K), 1)
    return pltpu.roll(jnp.where(j >= s, total[0:1], total[1:2]), (K - s) & (K - 1), axis=1)


def kernel(
    step_in, noise_seed_in, proj_seed_in, example_in, latent_ref, time_ref, w1_ref, w2_ref,
    section_ref, out_ref,
    stage, tall, side_in, corner_in, weight, actx, side_lhs, noise_keep, noisy_keep,
    hid_near, hid_far, cot_near, cot_far,
    lhs, s1, r1a, r1b, r1, s2, r2, s3, r3, row, grow, acc, bits,
    sum8, sum16, step_ref, noise_seed_ref, proj_seed_ref, example_ref, scalar_sem,
    load_sem, rim_send, rim_recv,
    pair_send, pair_recv, ring_send, ring_recv, two_send, two_recv, tail_send, tail_recv, all_send, all_recv,
):
    at = place()
    r_index = lax.axis_index("row")
    c_index = lax.axis_index("col")
    peers = peers_of(at)
    around = []
    for dr in (-1, 0, 1):
        for dc in (-1, 0, 1):
            if dr or dc:
                around.append((dr, dc))

    def beside(dr, dc):
        return (lax.rem(r_index + (16 + dr), 16), lax.rem(c_index + (8 + dc), 8))

    barrier = pltpu.get_barrier_semaphore()
    greeted = peers + [beside(dr, dc) for dr, dc in around]
    for peer in greeted:
        pl.semaphore_signal(barrier, inc=1, device_id=peer, device_id_type=MESH)

    def load(source, part):
        rows = pl.ds(part * THIRD, THIRD)
        return pltpu.make_async_copy(source.at[rows], weight.at[rows], load_sem.at[part])

    scalars = []
    for index, (source, held) in enumerate((
        (step_in, step_ref), (noise_seed_in, noise_seed_ref),
        (proj_seed_in, proj_seed_ref), (example_in, example_ref),
    )):
        scalars.append(pltpu.make_async_copy(source, held, scalar_sem.at[index]))
        scalars[-1].start()
    for part in range(3):
        load(w1_ref, part).start()
    for copy in scalars:
        copy.wait()

    salt = mix_bits(proj_seed_ref[0] + jnp.int32(12345))
    owner = ((at["core"] * 4 + at["x"]) * 4 + at["y"]) * 4 + at["z"]
    marks = [0]

    def fill(count):
        low = marks[-1]
        high = min(low + count, PADDED // 256)
        marks.append(high)
        if high > low:
            make_signs(salt, owner * RUN, bits, low, high)

    def pack(cells):
        rows = [f32(latent_ref[0, r])[c : c + 1] for r, c in cells]
        if len(rows) < 16:
            rows.append(jnp.zeros((16 - len(rows), CH), jnp.float32))
        return rounded(jnp.concatenate(rows, axis=0))

    edge = {-1: (0, 1), 1: (TW - 2, TW - 1)}
    brim = {-1: (0, 1), 1: (TH - 2, TH - 1)}
    for index, dc in enumerate((-1, 1)):
        stage[index] = pack([(r, c) for c in edge[dc] for r in range(TH)])
        for other, dr in enumerate((-1, 1)):
            stage[2 + other * 2 + index] = pack([(r, c) for c in edge[dc] for r in brim[dr]])

    example = example_ref[0]
    noise_salt = mix_bits(noise_seed_ref[0])
    row_first = r_index * TH
    col_first = c_index * TW
    when = jnp.broadcast_to(step_ref[0], (1, CH)).astype(jnp.float32)
    abar = jnp.cos((when / 1000.0 + 0.008) / 1.008 * (math.pi / 2.0)) ** 2
    keep = jnp.sqrt(abar)
    spoil = jnp.sqrt(1.0 - abar)
    col_here = lax.broadcasted_iota(jnp.int32, (TW, 1), 0)

    def noised(latent, rows, cols):
        noise = field(rows, cols, example, noise_salt)
        noisy = rounded(keep * f32(latent) + spoil * noise)
        act = f32(rounded(silu(f32(noisy))))
        return noise, noisy, act

    def middle(r):
        latent = latent_ref[0, r]
        noise, noisy, act = noised(latent, col_here * 0 + (row_first + r), col_first + col_here)
        noise_keep[r] = noise
        noisy_keep[r] = noisy
        actx[r + 2, :, CH : 2 * CH] = rounded(act)

    def middles(r, carry):
        middle(r)
        return carry

    fill(FILLS[0])
    pl.semaphore_wait(barrier, len(greeted))

    def send(src, dst, send_sem, recv_sem, to):
        copy = pltpu.make_async_remote_copy(
            src_ref=src, dst_ref=dst, send_sem=send_sem, recv_sem=recv_sem,
            device_id=to, device_id_type=MESH,
        )
        copy.start()
        return copy

    rims = []
    for index, (dr, dc) in enumerate(around):
        if dc == 0:
            src = latent_ref.at[0, pl.ds(brim[dr][0], 2)]
            dst = tall.at[0 if dr > 0 else 1]
        elif dr == 0:
            src = stage.at[0 if dc < 0 else 1]
            dst = side_in.at[0 if dc > 0 else 1]
        else:
            src = stage.at[2 + (0 if dr < 0 else 2) + (0 if dc < 0 else 1)]
            dst = corner_in.at[(0 if dr > 0 else 2) + (0 if dc > 0 else 1)]
        rims.append(send(src, dst, rim_send.at[index], rim_recv.at[index], beside(dr, dc)))
    started = list(rims)

    lax.fori_loop(0, TH, middles, 0)

    lane = lax.broadcasted_iota(jnp.int32, (1, CH), 1)
    half = jnp.where(lane < CH // 2, lane, lane - CH // 2)
    angle = when * jnp.exp(f32(half) * (-math.log(10000.0)) / (CH // 2))
    wave = jnp.where(lane < CH // 2, jnp.sin(angle), jnp.cos(angle))
    wave = rounded(jnp.concatenate([wave, jnp.zeros((15, CH), jnp.float32)], axis=0))
    temb = jnp.dot(wave, time_ref[...], preferred_element_type=jnp.float32)[0:1]
    fill(FILLS[1])
    for copy in rims:
        copy.wait_recv()

    def outer(which, r, grid_row):
        rows = col_here * 0 + grid_row
        cols = col_first + col_here
        act = noised(tall[which, r], rows, cols)[2]
        return jnp.where(inside(rows, cols), act, 0.0)

    for which, first in ((0, -2), (1, TH)):
        for r in range(2):
            act = outer(which, r, row_first + (first + r))
            actx[first + 2 + r, :, CH : 2 * CH] = rounded(act)
    flank = lax.broadcasted_iota(jnp.int32, (16, 1), 0)
    sides = []
    for index, first in enumerate((-2, TW)):
        rows = row_first + (flank & 7)
        cols = col_first + first + shift_right(flank, 3)
        act = noised(side_in[index], rows, cols)[2]
        sides.append(jnp.where(inside(rows, cols), act, 0.0))
    corners = jnp.concatenate([f32(corner_in[index])[0:4] for index in range(4)], axis=0)
    kind = shift_right(flank, 2)
    rows = row_first + (flank & 1) + jnp.where(kind < 2, -2, TH)
    cols = col_first + (shift_right(flank, 1) & 1) + jnp.where((kind & 1) == 0, -2, TW)
    corners = jnp.where(inside(rows, cols), noised(corners, rows, cols)[2], 0.0)

    def column(side, which):
        top = corners[4 * side + 2 * which : 4 * side + 2 * which + 2]
        bottom = corners[8 + 4 * side + 2 * which : 8 + 4 * side + 2 * which + 2]
        return jnp.concatenate([top, sides[side][8 * which : 8 * which + 8], bottom], axis=0)

    centre = [f32(actx[r, :, CH : 2 * CH]) for r in range(TH + 4)]
    lefts = [column(0, 0), column(0, 1), jnp.concatenate([c[0:1] for c in centre], axis=0)]
    rights = [jnp.concatenate([c[TW - 1 : TW] for c in centre], axis=0), column(1, 0), column(1, 1)]
    for r in range(TH + 4):
        cell = centre[r]
        actx[r, :, 0:CH] = rounded(
            jnp.where(col_here == 0, lefts[1][r : r + 1], pltpu.roll(cell, 1, axis=0))
        )
        actx[r, :, 2 * CH : 3 * CH] = rounded(
            jnp.where(col_here == TW - 1, rights[1][r : r + 1], pltpu.roll(cell, TW - 1, axis=0))
        )
    for dy in range(3):
        for dx in range(3):
            both = [lefts[dx][dy : dy + 10], rights[dx][dy : dy + 10], jnp.zeros((12, CH), jnp.float32)]
            side_lhs[dy, :, dx * CH : (dx + 1) * CH] = rounded(jnp.concatenate(both, axis=0))

    total = None
    for dy in range(3):
        load(w1_ref, dy).wait()
        left = jnp.concatenate(
            [actx[dy : dy + TH + 2].reshape((TH + 2) * TW, THIRD), side_lhs[dy]], axis=0
        )
        part = jnp.dot(left, weight[dy * THIRD : (dy + 1) * THIRD], preferred_element_type=jnp.float32)
        total = part if total is None else total + part
        load(w2_ref, dy).start()
    hidden = silu(total + temb)
    flanks = hidden[(TH + 2) * TW :]
    flank = lax.broadcasted_iota(jnp.int32, (32, 1), 0)
    right_side = jnp.where(flank < 10, 0, 1)
    rows = row_first - 1 + flank - right_side * 10
    cols = col_first - 1 + right_side * (TW + 1)
    flanks = jnp.where(inside(rows, cols), flanks, 0.0)
    for r in range(TH + 2):
        cell = hidden[r * TW : (r + 1) * TW]
        if r in (0, TH + 1):
            rows = col_here * 0 + (row_first + (r - 1))
            cell = jnp.where(inside(rows, col_first + col_here), cell, 0.0)
        hid_near[r, :, CH : 2 * CH] = rounded(cell)
        hid_near[r, :, 0:CH] = rounded(
            jnp.where(col_here == 0, flanks[r : r + 1], pltpu.roll(cell, 1, axis=0))
        )
        hid_near[r, :, 2 * CH : 3 * CH] = rounded(
            jnp.where(col_here == TW - 1, flanks[10 + r : 11 + r], pltpu.roll(cell, TW - 1, axis=0))
        )

    partner = device(at, core=lax.rem(at["core"] + 1, 2))
    pair = [send(hid_near, hid_far, pair_send.at[1], pair_recv.at[1], partner)]
    fill(FILLS[2])

    total = None
    for dy in range(3):
        load(w2_ref, dy).wait()
        part = jnp.dot(
            hid_near[dy : dy + TH].reshape(TH * TW, THIRD), weight[dy * THIRD : (dy + 1) * THIRD],
            preferred_element_type=jnp.float32,
        )
        total = part if total is None else total + part
    for r in range(TH):
        full = f32(noisy_keep[r]) + total[r * TW : (r + 1) * TW]
        section_ref[0, r] = rounded(full)
        cot_near[r * TW : (r + 1) * TW] = rounded((full - noise_keep[r]) * (1.0 / math.sqrt(ROWS * COLS)))
    pair.append(send(cot_near, cot_far, pair_send.at[0], pair_recv.at[0], partner))
    started += pair
    picks = [selection(third, at["core"]) for third in range(3)]

    def gather(side, cot):
        for third in range(3):
            lhs[third, side] = lax.dot_general(
                picks[third], cot[...], (((1,), (1,)), ((), ())), preferred_element_type=jnp.float32
            ).astype(jnp.bfloat16)

    gather(0, cot_near)
    for copy in pair:
        copy.wait_recv()
    gather(1, cot_far)

    def ring_one(third, level, blocks, ra, rb):
        axis = ORDERS[third][level]
        mine = at[axis]
        up = device(at, **{axis: hop(at, axis, 1)})
        down = device(at, **{axis: hop(at, axis, -1)})
        across = hop(at, axis, 2)
        sems = (third, level)
        return [
            send(blocks.at[third, across, :, pl.ds(0, CUT)], ra.at[third],
                 ring_send.at[third, level, 0], ring_recv.at[third, level, 0], up),
            send(blocks.at[third, across, :, pl.ds(CUT, THIRD - CUT)], rb.at[third],
                 ring_send.at[third, level, 1], ring_recv.at[third, level, 1], down),
        ]

    def ring_two(third, level, blocks, ra, rb, first, landed):
        axis = ORDERS[third][level]
        above = hop(at, axis, 1)
        below = hop(at, axis, -1)
        first[0].wait_recv()
        old = blocks[third, above, :, 0:CUT]
        blocks[third, above, :, 0:CUT] = (f32(old) + f32(ra[third])).astype(jnp.bfloat16)
        up = send(blocks.at[third, above], landed.at[third, 0],
                  ring_send.at[third, level, 2], ring_recv.at[third, level, 2],
                  device(at, **{axis: above}))
        first[1].wait_recv()
        old = blocks[third, below, :, CUT:THIRD]
        blocks[third, below, :, CUT:THIRD] = (f32(old) + f32(rb[third])).astype(jnp.bfloat16)
        down = send(blocks.at[third, below], landed.at[third, 1],
                    ring_send.at[third, level, 3], ring_recv.at[third, level, 3],
                    device(at, **{axis: below}))
        return [up, down]

    ones = []
    for third in range(3):
        near = hid_near[third : third + TH].reshape(TH * TW, THIRD)
        far = hid_far[third : third + TH].reshape(TH * TW, THIRD)
        total = jnp.dot(lhs[third, 0], near, preferred_element_type=jnp.float32)
        total += jnp.dot(lhs[third, 1], far, preferred_element_type=jnp.float32)
        s1[third] = rounded(total).reshape(4, 80, THIRD)
        ones.append(ring_one(third, 0, s1, r1a, r1b))
    fill(FILLS[3])
    twos = [ring_two(t, 0, s1, r1a, r1b, ones[t], r1) for t in range(3)]
    started += [copy for group in ones + twos for copy in group]
    fill(FILLS[4])
    def spread(third, level, blocks, landed, sends, recvs):
        axis = ORDERS[third][level]
        group = []
        for step in range(1, 4):
            to = hop(at, axis, step)
            group.append(
                send(blocks.at[third, to], landed.at[third, step - 1],
                     sends.at[third, step - 1], recvs.at[third, step - 1], device(at, **{axis: to}))
            )
        return group

    def gathered(third, level, blocks, landed, group):
        for copy in group:
            copy.wait_recv()
        total = f32(blocks[third, at[ORDERS[third][level]]])
        for index in range(3):
            total = total + f32(landed[third, index])
        return total

    seconds = []
    for third in range(3):
        mine = at[ORDERS[third][0]]
        for copy in twos[third]:
            copy.wait_recv()
        total = f32(s1[third, mine]) + f32(r1[third, 0]) + f32(r1[third, 1])
        for block in range(4):
            pieces = [
                total[block * 20 : block * 20 + 20, tile * 128 : tile * 128 + 128] for tile in range(TILES)
            ]
            pieces.append(jnp.zeros((4, 128), jnp.float32))
            s2[third, block] = rounded(jnp.concatenate(pieces, axis=0))
        seconds.append(spread(third, 1, s2, r2, two_send, two_recv))
    fill(FILLS[5])
    thirds = []
    for third in range(3):
        total = gathered(third, 1, s2, r2, seconds[third])
        for block in range(4):
            pieces = []
            for tile in range(TILES):
                first = tile * 20 + block * OWN
                pieces.append(total[first : first + OWN])
            pieces.append(jnp.zeros((5, 128), jnp.float32))
            s3[third, block] = rounded(jnp.concatenate(pieces, axis=0))
        thirds.append(spread(third, 2, s3, r3, tail_send, tail_recv))
    started += [copy for group in seconds + thirds for copy in group]
    fill(PADDED)
    row[...] = jnp.zeros_like(row)
    for third in range(3):
        total = gathered(third, 2, s3, r3, thirds[third])
        for tile in range(TILES):
            for channel in range(OWN):
                lanes = pl.ds(channel * TAPS + third * THIRD + tile * 128, 128)
                row[0:1, lanes] = total[tile * OWN + channel : tile * OWN + channel + 1]

    share = project(salt, owner * RUN, row, grow, bits, acc)

    share = share * (1.0 / math.sqrt(9.0 * CH * CH))
    for slots, me, first, count in (
        (sum8, at["x"] * 2 + at["core"], 0, 7),
        (sum16, at["y"] * 4 + at["z"], 7, 15),
    ):
        slots[me] = share
        group = []
        for index in range(first, first + count):
            group.append(send(slots.at[me], slots.at[me], all_send.at[index], all_recv.at[index], peers[index]))
        for copy in group:
            copy.wait_recv()
        started += group
        share = slots[0]
        for index in range(1, count + 1):
            share = share + slots[index]
    out_ref[...] = share
    for copy in started:
        copy.wait_send()


def call(step, noise_seed, proj_seed, example, latent, time_weight, w1, w2):
    bf16, full = jnp.bfloat16, jnp.float32
    vmem = pltpu.VMEM
    dma = pltpu.SemaphoreType.DMA
    scalar = pl.BlockSpec(memory_space=pl.ANY)
    near = pl.BlockSpec(memory_space=pltpu.VMEM)
    return pl.pallas_call(
        kernel,
        out_shape=(
            jax.ShapeDtypeStruct(latent.shape, bf16),
            jax.ShapeDtypeStruct((1, K), full),
        ),
        in_specs=[scalar] * 4 + [near] * 2 + [pl.BlockSpec(memory_space=pl.ANY)] * 2,
        out_specs=(near, near),
        scratch_shapes=[
            vmem((6, 16, CH), bf16),
            vmem((2, 2, TW, CH), bf16),
            vmem((2, 16, CH), bf16),
            vmem((4, 16, CH), bf16),
            vmem((TAPS, CH), bf16),
            vmem((TH + 4, TW, THIRD), bf16),
            vmem((3, 32, THIRD), bf16),
            vmem((TH, TW, CH), full),
            vmem((TH, TW, CH), bf16),
            vmem((TH + 2, TW, THIRD), bf16),
            vmem((TH + 2, TW, THIRD), bf16),
            vmem((TH * TW, CH), bf16),
            vmem((TH * TW, CH), bf16),
            vmem((3, 2, 320, 256), bf16),
            vmem((3, 4, 80, THIRD), bf16),
            vmem((3, 80, CUT), bf16),
            vmem((3, 80, THIRD - CUT), bf16),
            vmem((3, 2, 80, THIRD), bf16),
            vmem((3, 4, 304, 128), bf16),
            vmem((3, 3, 304, 128), bf16),
            vmem((3, 4, 80, 128), bf16),
            vmem((3, 3, 80, 128), bf16),
            vmem((1, PADDED), full),
            vmem((32, PADDED), F8),
            vmem((32, K), full),
            vmem((PADDED, K), F8),
            vmem((8, 1, K), full),
            vmem((16, 1, K), full),
            pltpu.SMEM((1,), jnp.int32),
            pltpu.SMEM((1,), jnp.int32),
            pltpu.SMEM((1,), jnp.int32),
            pltpu.SMEM((1,), jnp.int32),
            dma((4,)),
            dma((3,)),
            dma((8,)), dma((8,)),
            dma((2,)), dma((2,)),
            dma((3, 2, 4)), dma((3, 2, 4)),
            dma((3, 3)), dma((3, 3)),
            dma((3, 3)), dma((3, 3)),
            dma((22,)), dma((22,)),
        ],
        compiler_params=pltpu.CompilerParams(
            collective_id=0, has_side_effects=True, vmem_limit_bytes=60 * 2**20
        ),
    )(step, noise_seed, proj_seed, example, latent, time_weight, w1, w2)


def on_device(
    latent, timestep, noise_seed, proj_seed, example_ids, time_weight, conv1_weight, conv2_weight
):
    return call(
        timestep, noise_seed, proj_seed, example_ids, latent, time_weight, conv1_weight, conv2_weight
    )


def solution(mesh):
    placed = (P(None, "row", "col", None), P(), P(), P(), P(), P(), P(), P())
    return jax.shard_map(
        on_device,
        mesh=mesh,
        in_specs=placed,
        out_specs=(P(None, "row", "col", None), P()),
        check_vma=False,
    )
```

```python
import functools
import math

import jax
import jax.numpy as jnp
from jax import lax
from jax.experimental import pallas as pl
from jax.experimental.pallas import tpu as pltpu
from jax.sharding import PartitionSpec as P

K = 1024
FILLS = (8, 12, 0, 20, 30, 22)
M1 = 2146121005
M2 = -2073254261
MESH = pl.DeviceIdType.MESH


def wrap32(value):
    value &= 0xFFFFFFFF
    return value - (1 << 32) if value >= (1 << 31) else value


def mix_bits(value):
    value = value ^ lax.shift_right_logical(value, jnp.int32(16))
    value = value * jnp.int32(M1)
    value = value ^ lax.shift_right_logical(value, jnp.int32(15))
    value = value * jnp.int32(M2)
    value = value ^ lax.shift_right_logical(value, jnp.int32(16))
    return value


CH = 640
ROWS = 128
COLS = 256
TH = 8
TW = 32
TAPS = 9 * CH
THIRD = 3 * CH
TILES = THIRD // 128
CUT = 1024
OWN = 5
RUN = OWN * TAPS
PADDED = 29184
BLOCK = 4864
F8 = jnp.float8_e4m3fn
PARTS = 4
ORDERS = (("x", "y", "z"), ("y", "z", "x"), ("z", "x", "y"))


def place():
    r = lax.axis_index("row")
    c = lax.axis_index("col")
    return {
        "core": lax.rem(r, 2),
        "x": lax.rem(r // 2, 4),
        "y": lax.rem(c, 2) * 2 + r // 8,
        "z": c // 2,
    }


def device(at, **moved):
    at = {**at, **moved}
    row = (lax.rem(at["y"], 2) * 4 + at["x"]) * 2 + at["core"]
    return (row, at["z"] * 2 + at["y"] // 2)


def hop(at, axis, by):
    return lax.rem(at[axis] + (by + 4), 4)


def peers_of(at):
    out = []
    for step in range(4):
        for flip in range(2):
            if step or flip:
                out.append(device(at, x=hop(at, "x", step), core=lax.rem(at["core"] + flip, 2)))
    for up in range(4):
        for deep in range(4):
            if up or deep:
                out.append(device(at, y=hop(at, "y", up), z=hop(at, "z", deep)))
    return out


def silu(value):
    return value / (1.0 + jnp.exp(-value))


def rounded(value):
    return value.astype(jnp.bfloat16)


def field(rows, cols, example, salt):
    lane = lax.broadcasted_iota(jnp.int32, (1, CH), 1)
    base = ((example * ROWS + rows) * COLS + cols) * (4 * CH) + salt
    base = base + lane * 4
    total = None
    for index in range(4):
        bits = shift_right(mix_bits(base + index), 8)
        total = bits if total is None else total + bits
    return (f32(total) * (1.0 / 16777216.0) - 2.0) * math.sqrt(3.0)


def inside(rows, cols):
    return (rows >= 0) & (rows < ROWS) & (cols >= 0) & (cols < COLS)


def selection(third, core):
    row = lax.broadcasted_iota(jnp.int32, (320, 1), 0)
    owner = lax.shift_right_logical(row * 52429, jnp.int32(18))
    channel = row - owner * OWN
    digits = (lax.shift_right_logical(owner, jnp.int32(4)), lax.shift_right_logical(owner, jnp.int32(2)) & 3, owner & 3)
    named = dict(zip(ORDERS[third], digits))
    wanted = ((core * 4 + named["x"]) * 4 + named["y"]) * 4 + named["z"]
    wanted = wanted * OWN + channel
    lane = lax.broadcasted_iota(jnp.int32, (320, CH), 1)
    return jnp.where(lane == wanted, 1.0, 0.0).astype(jnp.bfloat16)


def f32(value):
    return value.astype(jnp.float32)


def shift_right(value, by):
    return lax.shift_right_logical(value, jnp.int32(by))


def alignment(salt, first):
    m_first = (first + shift_right(salt, 10)) & jnp.int32((1 << 22) - 1)
    ahead = m_first & 255
    return ahead, shift_right(m_first - ahead, 6)


def make_signs(salt, first, bits, low, high):
    h_first = alignment(salt, first)[1]
    lane = lax.broadcasted_iota(jnp.int32, (1, 128), 1)
    m_row = lax.broadcasted_iota(jnp.int32, (32, 128), 0)

    def body(step, carry):
        h_four = (h_first + step * 4) & 65535
        high_bits = shift_right(h_four, 10)
        columns = [((m_row + half) ^ high_bits) * jnp.int32(wrap32(1024 * M1)) for half in (0, 32)]
        for part in range(4):
            h = h_four + part
            for j in range(0, K, 128):
                line = ((lane + j) ^ (h & 1023)) * jnp.int32(M1) + h * jnp.int32(wrap32(65536 * M1))
                line = jnp.broadcast_to(line, (32, 128))
                for half in range(2):
                    w = line + columns[half]
                    y = (w ^ shift_right(w, 15)) * jnp.int32(M2)
                    rows = step * 256 + part * 64 + half * 32
                    rows = pl.ds(pl.multiple_of(rows, 32), 32)
                    bits[rows, j : j + 128] = lax.shift_right_arithmetic(y, 31).astype(jnp.int8).astype(F8)
        return carry

    lax.fori_loop(low, high, body, 0)


def project(salt, first, row, grow, bits, acc):
    s = salt & (K - 1)
    ahead = alignment(salt, first)[0]
    flat = row[...]
    whole = jnp.sum(flat)
    largest = jnp.maximum(jnp.max(jnp.abs(flat)), 1e-30)
    one = pltpu.roll(flat * (16.0 / largest), ahead, axis=1)
    two = pltpu.roll(one, 1, axis=1)
    for block in range(PADDED // BLOCK):
        lanes = slice(block * BLOCK, (block + 1) * BLOCK)
        pair = jnp.concatenate([one[:, lanes], two[:, lanes]], axis=0)
        pieces = []
        for _ in range(PARTS):
            piece = lax.round(pair, lax.RoundingMethod.TO_NEAREST_EVEN)
            pieces.append(piece)
            pair = (pair - piece) * 32.0
        pieces.append(jnp.zeros((24, BLOCK), jnp.float32))
        grow[:, lanes] = jnp.concatenate(pieces, axis=0).astype(F8)
    acc[...] = jnp.zeros_like(acc)

    def body(step, carry):
        lanes = pl.ds(pl.multiple_of(step * BLOCK, BLOCK), BLOCK)
        acc[...] += jnp.dot(grow[:, lanes], bits[lanes, :], preferred_element_type=jnp.float32)
        return carry

    lax.fori_loop(0, PADDED // BLOCK, body, 0)
    total = acc[6:8, :]
    for index in (2, 1, 0):
        total = acc[2 * index : 2 * index + 2, :] + total * (1.0 / 32.0)
    total = whole + total * (largest * (2.0 / 16.0))
    j = lax.broadcasted_iota(jnp.int32, (1, K), 1)
    return pltpu.roll(jnp.where(j >= s, total[0:1], total[1:2]), (K - s) & (K - 1), axis=1)


def kernel(
    step_in, noise_seed_in, proj_seed_in, example_in, latent_in, time_in, w1_ref, w2_ref,
    section_out, out_ref,
    stage, tall, side_in, corner_in, weight, actx, side_lhs, noise_keep, noisy_keep,
    hid_near, hid_far, cot_near, cot_far,
    lhs, s1, r1a, r1b, r1, s2, r2, s3, r3, row, grow, acc, bits,
    sum8, sum16, step_ref, noise_seed_ref, proj_seed_ref, example_ref, scalar_sem,
    latent_ref, time_ref, section_ref, whole_sem,
    load_sem, rim_send, rim_recv,
    pair_send, pair_recv, ring_send, ring_recv, two_send, two_recv, tail_send, tail_recv, all_send, all_recv,
):
    at = place()
    r_index = lax.axis_index("row")
    c_index = lax.axis_index("col")
    peers = peers_of(at)
    around = []
    for dr in (-1, 0, 1):
        for dc in (-1, 0, 1):
            if dr or dc:
                around.append((dr, dc))

    def beside(dr, dc):
        return (lax.rem(r_index + (16 + dr), 16), lax.rem(c_index + (8 + dc), 8))

    barrier = pltpu.get_barrier_semaphore()
    greeted = peers + [beside(dr, dc) for dr, dc in around]
    for peer in greeted:
        pl.semaphore_signal(barrier, inc=1, device_id=peer, device_id_type=MESH)

    def load(source, part):
        rows = pl.ds(part * THIRD, THIRD)
        return pltpu.make_async_copy(source.at[rows], weight.at[rows], load_sem.at[part])

    latent_copy = pltpu.make_async_copy(latent_in, latent_ref, whole_sem.at[0])
    latent_copy.start()
    scalars = []
    for index, (source, held) in enumerate((
        (step_in, step_ref), (noise_seed_in, noise_seed_ref),
        (proj_seed_in, proj_seed_ref), (example_in, example_ref),
    )):
        scalars.append(pltpu.make_async_copy(source, held, scalar_sem.at[index]))
        scalars[-1].start()
    for part in range(3):
        load(w1_ref, part).start()
    time_copy = pltpu.make_async_copy(time_in, time_ref, whole_sem.at[1])
    time_copy.start()
    for copy in scalars:
        copy.wait()

    salt = mix_bits(proj_seed_ref[0] + jnp.int32(12345))
    owner = ((at["core"] * 4 + at["x"]) * 4 + at["y"]) * 4 + at["z"]
    marks = [0]

    def fill(count):
        low = marks[-1]
        high = min(low + count, PADDED // 256)
        marks.append(high)
        if high > low:
            make_signs(salt, owner * RUN, bits, low, high)

    def pack(cells):
        rows = [f32(latent_ref[0, r])[c : c + 1] for r, c in cells]
        if len(rows) < 16:
            rows.append(jnp.zeros((16 - len(rows), CH), jnp.float32))
        return rounded(jnp.concatenate(rows, axis=0))

    latent_copy.wait()
    edge = {-1: (0, 1), 1: (TW - 2, TW - 1)}
    brim = {-1: (0, 1), 1: (TH - 2, TH - 1)}
    for index, dc in enumerate((-1, 1)):
        stage[index] = pack([(r, c) for c in edge[dc] for r in range(TH)])
        for other, dr in enumerate((-1, 1)):
            stage[2 + other * 2 + index] = pack([(r, c) for c in edge[dc] for r in brim[dr]])

    example = example_ref[0]
    noise_salt = mix_bits(noise_seed_ref[0])
    row_first = r_index * TH
    col_first = c_index * TW
    when = jnp.broadcast_to(step_ref[0], (1, CH)).astype(jnp.float32)
    abar = jnp.cos((when / 1000.0 + 0.008) / 1.008 * (math.pi / 2.0)) ** 2
    keep = jnp.sqrt(abar)
    spoil = jnp.sqrt(1.0 - abar)
    col_here = lax.broadcasted_iota(jnp.int32, (TW, 1), 0)

    def noised(latent, rows, cols):
        noise = field(rows, cols, example, noise_salt)
        noisy = rounded(keep * f32(latent) + spoil * noise)
        act = f32(rounded(silu(f32(noisy))))
        return noise, noisy, act

    def middle(r):
        latent = latent_ref[0, r]
        noise, noisy, act = noised(latent, col_here * 0 + (row_first + r), col_first + col_here)
        noise_keep[r] = noise
        noisy_keep[r] = noisy
        actx[r + 2, :, CH : 2 * CH] = rounded(act)

    def middles(r, carry):
        middle(r)
        return carry

    fill(FILLS[0])
    pl.semaphore_wait(barrier, len(greeted))

    def send(src, dst, send_sem, recv_sem, to):
        copy = pltpu.make_async_remote_copy(
            src_ref=src, dst_ref=dst, send_sem=send_sem, recv_sem=recv_sem,
            device_id=to, device_id_type=MESH,
        )
        copy.start()
        return copy

    rims = []
    for index, (dr, dc) in enumerate(around):
        if dc == 0:
            src = latent_ref.at[0, pl.ds(brim[dr][0], 2)]
            dst = tall.at[0 if dr > 0 else 1]
        elif dr == 0:
            src = stage.at[0 if dc < 0 else 1]
            dst = side_in.at[0 if dc > 0 else 1]
        else:
            src = stage.at[2 + (0 if dr < 0 else 2) + (0 if dc < 0 else 1)]
            dst = corner_in.at[(0 if dr > 0 else 2) + (0 if dc > 0 else 1)]
        rims.append(send(src, dst, rim_send.at[index], rim_recv.at[index], beside(dr, dc)))
    started = list(rims)

    lax.fori_loop(0, TH, middles, 0)

    lane = lax.broadcasted_iota(jnp.int32, (1, CH), 1)
    half = jnp.where(lane < CH // 2, lane, lane - CH // 2)
    angle = when * jnp.exp(f32(half) * (-math.log(10000.0)) / (CH // 2))
    wave = jnp.where(lane < CH // 2, jnp.sin(angle), jnp.cos(angle))
    wave = rounded(jnp.concatenate([wave, jnp.zeros((15, CH), jnp.float32)], axis=0))
    time_copy.wait()
    temb = jnp.dot(wave, time_ref[...], preferred_element_type=jnp.float32)[0:1]
    fill(FILLS[1])
    for copy in rims:
        copy.wait_recv()

    def outer(which, r, grid_row):
        rows = col_here * 0 + grid_row
        cols = col_first + col_here
        act = noised(tall[which, r], rows, cols)[2]
        return jnp.where(inside(rows, cols), act, 0.0)

    for which, first in ((0, -2), (1, TH)):
        for r in range(2):
            act = outer(which, r, row_first + (first + r))
            actx[first + 2 + r, :, CH : 2 * CH] = rounded(act)
    flank = lax.broadcasted_iota(jnp.int32, (16, 1), 0)
    sides = []
    for index, first in enumerate((-2, TW)):
        rows = row_first + (flank & 7)
        cols = col_first + first + shift_right(flank, 3)
        act = noised(side_in[index], rows, cols)[2]
        sides.append(jnp.where(inside(rows, cols), act, 0.0))
    corners = jnp.concatenate([f32(corner_in[index])[0:4] for index in range(4)], axis=0)
    kind = shift_right(flank, 2)
    rows = row_first + (flank & 1) + jnp.where(kind < 2, -2, TH)
    cols = col_first + (shift_right(flank, 1) & 1) + jnp.where((kind & 1) == 0, -2, TW)
    corners = jnp.where(inside(rows, cols), noised(corners, rows, cols)[2], 0.0)

    def column(side, which):
        top = corners[4 * side + 2 * which : 4 * side + 2 * which + 2]
        bottom = corners[8 + 4 * side + 2 * which : 8 + 4 * side + 2 * which + 2]
        return jnp.concatenate([top, sides[side][8 * which : 8 * which + 8], bottom], axis=0)

    centre = [f32(actx[r, :, CH : 2 * CH]) for r in range(TH + 4)]
    lefts = [column(0, 0), column(0, 1), jnp.concatenate([c[0:1] for c in centre], axis=0)]
    rights = [jnp.concatenate([c[TW - 1 : TW] for c in centre], axis=0), column(1, 0), column(1, 1)]
    for r in range(TH + 4):
        cell = centre[r]
        actx[r, :, 0:CH] = rounded(
            jnp.where(col_here == 0, lefts[1][r : r + 1], pltpu.roll(cell, 1, axis=0))
        )
        actx[r, :, 2 * CH : 3 * CH] = rounded(
            jnp.where(col_here == TW - 1, rights[1][r : r + 1], pltpu.roll(cell, TW - 1, axis=0))
        )
    for dy in range(3):
        for dx in range(3):
            both = [lefts[dx][dy : dy + 10], rights[dx][dy : dy + 10], jnp.zeros((12, CH), jnp.float32)]
            side_lhs[dy, :, dx * CH : (dx + 1) * CH] = rounded(jnp.concatenate(both, axis=0))

    total = None
    for dy in range(3):
        load(w1_ref, dy).wait()
        left = jnp.concatenate(
            [actx[dy : dy + TH + 2].reshape((TH + 2) * TW, THIRD), side_lhs[dy]], axis=0
        )
        part = jnp.dot(left, weight[dy * THIRD : (dy + 1) * THIRD], preferred_element_type=jnp.float32)
        total = part if total is None else total + part
        load(w2_ref, dy).start()
    hidden = silu(total + temb)
    flanks = hidden[(TH + 2) * TW :]
    flank = lax.broadcasted_iota(jnp.int32, (32, 1), 0)
    right_side = jnp.where(flank < 10, 0, 1)
    rows = row_first - 1 + flank - right_side * 10
    cols = col_first - 1 + right_side * (TW + 1)
    flanks = jnp.where(inside(rows, cols), flanks, 0.0)
    for r in range(TH + 2):
        cell = hidden[r * TW : (r + 1) * TW]
        if r in (0, TH + 1):
            rows = col_here * 0 + (row_first + (r - 1))
            cell = jnp.where(inside(rows, col_first + col_here), cell, 0.0)
        hid_near[r, :, CH : 2 * CH] = rounded(cell)
        hid_near[r, :, 0:CH] = rounded(
            jnp.where(col_here == 0, flanks[r : r + 1], pltpu.roll(cell, 1, axis=0))
        )
        hid_near[r, :, 2 * CH : 3 * CH] = rounded(
            jnp.where(col_here == TW - 1, flanks[10 + r : 11 + r], pltpu.roll(cell, TW - 1, axis=0))
        )

    partner = device(at, core=lax.rem(at["core"] + 1, 2))
    pair = [send(hid_near, hid_far, pair_send.at[1], pair_recv.at[1], partner)]
    fill(FILLS[2])

    total = None
    for dy in range(3):
        load(w2_ref, dy).wait()
        part = jnp.dot(
            hid_near[dy : dy + TH].reshape(TH * TW, THIRD), weight[dy * THIRD : (dy + 1) * THIRD],
            preferred_element_type=jnp.float32,
        )
        total = part if total is None else total + part
    for r in range(TH):
        full = f32(noisy_keep[r]) + total[r * TW : (r + 1) * TW]
        section_ref[0, r] = rounded(full)
        cot_near[r * TW : (r + 1) * TW] = rounded((full - noise_keep[r]) * (1.0 / math.sqrt(ROWS * COLS)))
    section_copy = pltpu.make_async_copy(section_ref, section_out, whole_sem.at[2])
    section_copy.start()
    pair.append(send(cot_near, cot_far, pair_send.at[0], pair_recv.at[0], partner))
    started += pair
    picks = [selection(third, at["core"]) for third in range(3)]

    def gather(side, cot):
        for third in range(3):
            lhs[third, side] = lax.dot_general(
                picks[third], cot[...], (((1,), (1,)), ((), ())), preferred_element_type=jnp.float32
            ).astype(jnp.bfloat16)

    gather(0, cot_near)
    for copy in pair:
        copy.wait_recv()
    gather(1, cot_far)

    def ring_one(third, level, blocks, ra, rb):
        axis = ORDERS[third][level]
        mine = at[axis]
        up = device(at, **{axis: hop(at, axis, 1)})
        down = device(at, **{axis: hop(at, axis, -1)})
        across = hop(at, axis, 2)
        sems = (third, level)
        return [
            send(blocks.at[third, across, :, pl.ds(0, CUT)], ra.at[third],
                 ring_send.at[third, level, 0], ring_recv.at[third, level, 0], up),
            send(blocks.at[third, across, :, pl.ds(CUT, THIRD - CUT)], rb.at[third],
                 ring_send.at[third, level, 1], ring_recv.at[third, level, 1], down),
        ]

    def ring_two(third, level, blocks, ra, rb, first, landed):
        axis = ORDERS[third][level]
        above = hop(at, axis, 1)
        below = hop(at, axis, -1)
        first[0].wait_recv()
        old = blocks[third, above, :, 0:CUT]
        blocks[third, above, :, 0:CUT] = (f32(old) + f32(ra[third])).astype(jnp.bfloat16)
        up = send(blocks.at[third, above], landed.at[third, 0],
                  ring_send.at[third, level, 2], ring_recv.at[third, level, 2],
                  device(at, **{axis: above}))
        first[1].wait_recv()
        old = blocks[third, below, :, CUT:THIRD]
        blocks[third, below, :, CUT:THIRD] = (f32(old) + f32(rb[third])).astype(jnp.bfloat16)
        down = send(blocks.at[third, below], landed.at[third, 1],
                    ring_send.at[third, level, 3], ring_recv.at[third, level, 3],
                    device(at, **{axis: below}))
        return [up, down]

    ones = []
    for third in range(3):
        near = hid_near[third : third + TH].reshape(TH * TW, THIRD)
        far = hid_far[third : third + TH].reshape(TH * TW, THIRD)
        total = jnp.dot(lhs[third, 0], near, preferred_element_type=jnp.float32)
        total += jnp.dot(lhs[third, 1], far, preferred_element_type=jnp.float32)
        s1[third] = rounded(total).reshape(4, 80, THIRD)
        ones.append(ring_one(third, 0, s1, r1a, r1b))
    fill(FILLS[3])
    twos = [ring_two(t, 0, s1, r1a, r1b, ones[t], r1) for t in range(3)]
    started += [copy for group in ones + twos for copy in group]
    fill(FILLS[4])
    def spread(third, level, blocks, landed, sends, recvs):
        axis = ORDERS[third][level]
        group = []
        for step in range(1, 4):
            to = hop(at, axis, step)
            group.append(
                send(blocks.at[third, to], landed.at[third, step - 1],
                     sends.at[third, step - 1], recvs.at[third, step - 1], device(at, **{axis: to}))
            )
        return group

    def gathered(third, level, blocks, landed, group):
        for copy in group:
            copy.wait_recv()
        total = f32(blocks[third, at[ORDERS[third][level]]])
        for index in range(3):
            total = total + f32(landed[third, index])
        return total

    seconds = []
    for third in range(3):
        mine = at[ORDERS[third][0]]
        for copy in twos[third]:
            copy.wait_recv()
        total = f32(s1[third, mine]) + f32(r1[third, 0]) + f32(r1[third, 1])
        for block in range(4):
            pieces = [
                total[block * 20 : block * 20 + 20, tile * 128 : tile * 128 + 128] for tile in range(TILES)
            ]
            pieces.append(jnp.zeros((4, 128), jnp.float32))
            s2[third, block] = rounded(jnp.concatenate(pieces, axis=0))
        seconds.append(spread(third, 1, s2, r2, two_send, two_recv))
    fill(FILLS[5])
    thirds = []
    for third in range(3):
        total = gathered(third, 1, s2, r2, seconds[third])
        for block in range(4):
            pieces = []
            for tile in range(TILES):
                first = tile * 20 + block * OWN
                pieces.append(total[first : first + OWN])
            pieces.append(jnp.zeros((5, 128), jnp.float32))
            s3[third, block] = rounded(jnp.concatenate(pieces, axis=0))
        thirds.append(spread(third, 2, s3, r3, tail_send, tail_recv))
    started += [copy for group in seconds + thirds for copy in group]
    fill(PADDED)
    row[...] = jnp.zeros_like(row)
    for third in range(3):
        total = gathered(third, 2, s3, r3, thirds[third])
        for tile in range(TILES):
            for channel in range(OWN):
                lanes = pl.ds(channel * TAPS + third * THIRD + tile * 128, 128)
                row[0:1, lanes] = total[tile * OWN + channel : tile * OWN + channel + 1]

    share = project(salt, owner * RUN, row, grow, bits, acc)

    share = share * (1.0 / math.sqrt(9.0 * CH * CH))
    for slots, me, first, count in (
        (sum8, at["x"] * 2 + at["core"], 0, 7),
        (sum16, at["y"] * 4 + at["z"], 7, 15),
    ):
        slots[me] = share
        group = []
        for index in range(first, first + count):
            group.append(send(slots.at[me], slots.at[me], all_send.at[index], all_recv.at[index], peers[index]))
        for copy in group:
            copy.wait_recv()
        started += group
        share = slots[0]
        for index in range(1, count + 1):
            share = share + slots[index]
    out_ref[...] = share
    section_copy.wait()
    for copy in started:
        copy.wait_send()


def call(step, noise_seed, proj_seed, example, latent, time_weight, w1, w2):
    bf16, full = jnp.bfloat16, jnp.float32
    vmem = pltpu.VMEM
    dma = pltpu.SemaphoreType.DMA
    far = pl.BlockSpec(memory_space=pl.ANY)
    return pl.pallas_call(
        kernel,
        out_shape=(
            jax.ShapeDtypeStruct(latent.shape, bf16),
            jax.ShapeDtypeStruct((1, K), full),
        ),
        in_specs=[far] * 8,
        out_specs=(far, pl.BlockSpec(memory_space=pltpu.VMEM)),
        scratch_shapes=[
            vmem((6, 16, CH), bf16),
            vmem((2, 2, TW, CH), bf16),
            vmem((2, 16, CH), bf16),
            vmem((4, 16, CH), bf16),
            vmem((TAPS, CH), bf16),
            vmem((TH + 4, TW, THIRD), bf16),
            vmem((3, 32, THIRD), bf16),
            vmem((TH, TW, CH), full),
            vmem((TH, TW, CH), bf16),
            vmem((TH + 2, TW, THIRD), bf16),
            vmem((TH + 2, TW, THIRD), bf16),
            vmem((TH * TW, CH), bf16),
            vmem((TH * TW, CH), bf16),
            vmem((3, 2, 320, 256), bf16),
            vmem((3, 4, 80, THIRD), bf16),
            vmem((3, 80, CUT), bf16),
            vmem((3, 80, THIRD - CUT), bf16),
            vmem((3, 2, 80, THIRD), bf16),
            vmem((3, 4, 304, 128), bf16),
            vmem((3, 3, 304, 128), bf16),
            vmem((3, 4, 80, 128), bf16),
            vmem((3, 3, 80, 128), bf16),
            vmem((1, PADDED), full),
            vmem((32, PADDED), F8),
            vmem((32, K), full),
            vmem((PADDED, K), F8),
            vmem((8, 1, K), full),
            vmem((16, 1, K), full),
            pltpu.SMEM((1,), jnp.int32),
            pltpu.SMEM((1,), jnp.int32),
            pltpu.SMEM((1,), jnp.int32),
            pltpu.SMEM((1,), jnp.int32),
            dma((4,)),
            vmem(latent.shape, bf16),
            vmem(time_weight.shape, bf16),
            vmem(latent.shape, bf16),
            dma((3,)),
            dma((3,)),
            dma((8,)), dma((8,)),
            dma((2,)), dma((2,)),
            dma((3, 2, 4)), dma((3, 2, 4)),
            dma((3, 3)), dma((3, 3)),
            dma((3, 3)), dma((3, 3)),
            dma((22,)), dma((22,)),
        ],
        compiler_params=pltpu.CompilerParams(
            collective_id=0, has_side_effects=True, vmem_limit_bytes=60 * 2**20
        ),
    )(step, noise_seed, proj_seed, example, latent, time_weight, w1, w2)


def on_device(
    latent, timestep, noise_seed, proj_seed, example_ids, time_weight, conv1_weight, conv2_weight
):
    return call(
        timestep, noise_seed, proj_seed, example_ids, latent, time_weight, conv1_weight, conv2_weight
    )


def solution(mesh):
    placed = (P(None, "row", "col", None), P(), P(), P(), P(), P(), P(), P())
    return jax.shard_map(
        on_device,
        mesh=mesh,
        in_specs=placed,
        out_specs=(P(None, "row", "col", None), P()),
        check_vma=False,
    )
```

```python
import functools
import math

import jax
import jax.numpy as jnp
from jax import lax
from jax.experimental import pallas as pl
from jax.experimental.pallas import tpu as pltpu
from jax.sharding import PartitionSpec as P

K = 1024
FILLS = (8, 12, 0, 20, 30, 22)
M1 = 2146121005
M2 = -2073254261
MESH = pl.DeviceIdType.MESH


def wrap32(value):
    value &= 0xFFFFFFFF
    return value - (1 << 32) if value >= (1 << 31) else value


def mix_bits(value):
    value = value ^ lax.shift_right_logical(value, jnp.int32(16))
    value = value * jnp.int32(M1)
    value = value ^ lax.shift_right_logical(value, jnp.int32(15))
    value = value * jnp.int32(M2)
    value = value ^ lax.shift_right_logical(value, jnp.int32(16))
    return value


CH = 640
ROWS = 128
COLS = 256
TH = 8
TW = 32
TAPS = 9 * CH
THIRD = 3 * CH
TILES = THIRD // 128
CUT = 1024
OWN = 5
RUN = OWN * TAPS
PADDED = 29184
BLOCK = 4864
F8 = jnp.float8_e4m3fn
PARTS = 4
ORDERS = (("x", "y", "z"), ("y", "z", "x"), ("z", "x", "y"))


def place():
    r = lax.axis_index("row")
    c = lax.axis_index("col")
    return {
        "core": lax.rem(r, 2),
        "x": lax.rem(r // 2, 4),
        "y": lax.rem(c, 2) * 2 + r // 8,
        "z": c // 2,
    }


def device(at, **moved):
    at = {**at, **moved}
    row = (lax.rem(at["y"], 2) * 4 + at["x"]) * 2 + at["core"]
    return (row, at["z"] * 2 + at["y"] // 2)


def hop(at, axis, by):
    return lax.rem(at[axis] + (by + 4), 4)


def peers_of(at):
    out = []
    for step in range(4):
        for flip in range(2):
            if step or flip:
                out.append(device(at, x=hop(at, "x", step), core=lax.rem(at["core"] + flip, 2)))
    for up in range(4):
        for deep in range(4):
            if up or deep:
                out.append(device(at, y=hop(at, "y", up), z=hop(at, "z", deep)))
    return out


def silu(value):
    return value / (1.0 + jnp.exp(-value))


def rounded(value):
    return value.astype(jnp.bfloat16)


def field(rows, cols, example, salt):
    lane = lax.broadcasted_iota(jnp.int32, (1, CH), 1)
    base = ((example * ROWS + rows) * COLS + cols) * (4 * CH) + salt
    base = base + lane * 4
    total = None
    for index in range(4):
        bits = shift_right(mix_bits(base + index), 8)
        total = bits if total is None else total + bits
    return (f32(total) * (1.0 / 16777216.0) - 2.0) * math.sqrt(3.0)


def inside(rows, cols):
    return (rows >= 0) & (rows < ROWS) & (cols >= 0) & (cols < COLS)


def selection(third, core):
    row = lax.broadcasted_iota(jnp.int32, (320, 1), 0)
    owner = lax.shift_right_logical(row * 52429, jnp.int32(18))
    channel = row - owner * OWN
    digits = (lax.shift_right_logical(owner, jnp.int32(4)), lax.shift_right_logical(owner, jnp.int32(2)) & 3, owner & 3)
    named = dict(zip(ORDERS[third], digits))
    wanted = ((core * 4 + named["x"]) * 4 + named["y"]) * 4 + named["z"]
    wanted = wanted * OWN + channel
    lane = lax.broadcasted_iota(jnp.int32, (320, CH), 1)
    return jnp.where(lane == wanted, 1.0, 0.0).astype(jnp.bfloat16)


def f32(value):
    return value.astype(jnp.float32)


def shift_right(value, by):
    return lax.shift_right_logical(value, jnp.int32(by))


def alignment(salt, first):
    m_first = (first + shift_right(salt, 10)) & jnp.int32((1 << 22) - 1)
    ahead = m_first & 255
    return ahead, shift_right(m_first - ahead, 6)


def make_signs(salt, first, bits, low, high):
    h_first = alignment(salt, first)[1]
    lane = lax.broadcasted_iota(jnp.int32, (1, 128), 1)
    m_row = lax.broadcasted_iota(jnp.int32, (32, 128), 0)

    def body(step, carry):
        h_four = (h_first + step * 4) & 65535
        high_bits = shift_right(h_four, 10)
        columns = [((m_row + half) ^ high_bits) * jnp.int32(wrap32(1024 * M1)) for half in (0, 32)]
        for part in range(4):
            h = h_four + part
            for j in range(0, K, 128):
                line = ((lane + j) ^ (h & 1023)) * jnp.int32(M1) + h * jnp.int32(wrap32(65536 * M1))
                line = jnp.broadcast_to(line, (32, 128))
                for half in range(2):
                    w = line + columns[half]
                    y = (w ^ shift_right(w, 15)) * jnp.int32(M2)
                    rows = step * 256 + part * 64 + half * 32
                    rows = pl.ds(pl.multiple_of(rows, 32), 32)
                    bits[rows, j : j + 128] = lax.shift_right_arithmetic(y, 31).astype(jnp.int8).astype(F8)
        return carry

    lax.fori_loop(low, high, body, 0)


def project(salt, first, row, grow, bits, acc):
    s = salt & (K - 1)
    ahead = alignment(salt, first)[0]
    flat = row[...]
    whole = jnp.sum(flat)
    largest = jnp.maximum(jnp.max(jnp.abs(flat)), 1e-30)
    one = pltpu.roll(flat * (16.0 / largest), ahead, axis=1)
    two = pltpu.roll(one, 1, axis=1)
    for block in range(PADDED // BLOCK):
        lanes = slice(block * BLOCK, (block + 1) * BLOCK)
        pair = jnp.concatenate([one[:, lanes], two[:, lanes]], axis=0)
        pieces = []
        for _ in range(PARTS):
            piece = lax.round(pair, lax.RoundingMethod.TO_NEAREST_EVEN)
            pieces.append(piece)
            pair = (pair - piece) * 32.0
        pieces.append(jnp.zeros((24, BLOCK), jnp.float32))
        grow[:, lanes] = jnp.concatenate(pieces, axis=0).astype(F8)
    acc[...] = jnp.zeros_like(acc)

    def body(step, carry):
        lanes = pl.ds(pl.multiple_of(step * BLOCK, BLOCK), BLOCK)
        acc[...] += jnp.dot(grow[:, lanes], bits[lanes, :], preferred_element_type=jnp.float32)
        return carry

    lax.fori_loop(0, PADDED // BLOCK, body, 0)
    total = acc[6:8, :]
    for index in (2, 1, 0):
        total = acc[2 * index : 2 * index + 2, :] + total * (1.0 / 32.0)
    total = whole + total * (largest * (2.0 / 16.0))
    j = lax.broadcasted_iota(jnp.int32, (1, K), 1)
    return pltpu.roll(jnp.where(j >= s, total[0:1], total[1:2]), (K - s) & (K - 1), axis=1)


def kernel(
    step_in, noise_seed_in, proj_seed_in, example_in, latent_in, time_in, w1_ref, w2_ref,
    section_out, out_ref,
    stage, tall, side_in, corner_in, weight, actx, side_lhs, noise_keep, noisy_keep,
    hid_near, hid_far, cot_near, cot_far,
    lhs, s1, r1a, r1b, r1, s2, r2, s3, r3, row, grow, acc, bits,
    sum8, sum16, step_ref, noise_seed_ref, proj_seed_ref, example_ref, scalar_sem,
    latent_ref, time_ref, section_ref, whole_sem,
    load_sem, rim_send, rim_recv,
    pair_send, pair_recv, ring_send, ring_recv, two_send, two_recv, tail_send, tail_recv, all_send, all_recv,
):
    at = place()
    r_index = lax.axis_index("row")
    c_index = lax.axis_index("col")
    peers = peers_of(at)
    around = []
    for dr in (-1, 0, 1):
        for dc in (-1, 0, 1):
            if dr or dc:
                around.append((dr, dc))

    def beside(dr, dc):
        return (lax.rem(r_index + (16 + dr), 16), lax.rem(c_index + (8 + dc), 8))

    barrier = pltpu.get_barrier_semaphore()
    greeted = peers + [beside(dr, dc) for dr, dc in around]
    for peer in greeted:
        pl.semaphore_signal(barrier, inc=1, device_id=peer, device_id_type=MESH)

    def load(source, part):
        rows = pl.ds(part * THIRD, THIRD)
        return pltpu.make_async_copy(source.at[rows], weight.at[rows], load_sem.at[part])

    latent_copy = pltpu.make_async_copy(latent_in, latent_ref, whole_sem.at[0])
    latent_copy.start()
    scalars = []
    for index, (source, held) in enumerate((
        (step_in, step_ref), (noise_seed_in, noise_seed_ref),
        (proj_seed_in, proj_seed_ref), (example_in, example_ref),
    )):
        scalars.append(pltpu.make_async_copy(source, held, scalar_sem.at[index]))
        scalars[-1].start()
    for part in range(3):
        load(w1_ref, part).start()
    time_copy = pltpu.make_async_copy(time_in, time_ref, whole_sem.at[1])
    time_copy.start()
    for copy in scalars:
        copy.wait()

    salt = mix_bits(proj_seed_ref[0] + jnp.int32(12345))
    owner = ((at["core"] * 4 + at["x"]) * 4 + at["y"]) * 4 + at["z"]
    marks = [0]

    def fill(count):
        low = marks[-1]
        high = min(low + count, PADDED // 256)
        marks.append(high)
        if high > low:
            make_signs(salt, owner * RUN, bits, low, high)

    def pack(cells):
        rows = [f32(latent_ref[0, r])[c : c + 1] for r, c in cells]
        if len(rows) < 16:
            rows.append(jnp.zeros((16 - len(rows), CH), jnp.float32))
        return rounded(jnp.concatenate(rows, axis=0))

    latent_copy.wait()
    edge = {-1: (0, 1), 1: (TW - 2, TW - 1)}
    brim = {-1: (0, 1), 1: (TH - 2, TH - 1)}
    for index, dc in enumerate((-1, 1)):
        stage[index] = pack([(r, c) for c in edge[dc] for r in range(TH)])
        for other, dr in enumerate((-1, 1)):
            stage[2 + other * 2 + index] = pack([(r, c) for c in edge[dc] for r in brim[dr]])

    example = example_ref[0]
    noise_salt = mix_bits(noise_seed_ref[0])
    row_first = r_index * TH
    col_first = c_index * TW
    when = jnp.broadcast_to(step_ref[0], (1, CH)).astype(jnp.float32)
    abar = jnp.cos((when / 1000.0 + 0.008) / 1.008 * (math.pi / 2.0)) ** 2
    keep = jnp.sqrt(abar)
    spoil = jnp.sqrt(1.0 - abar)
    col_here = lax.broadcasted_iota(jnp.int32, (TW, 1), 0)

    def noised(latent, rows, cols):
        noise = field(rows, cols, example, noise_salt)
        noisy = rounded(keep * f32(latent) + spoil * noise)
        act = f32(rounded(silu(f32(noisy))))
        return noise, noisy, act

    def middle(r):
        latent = latent_ref[0, r]
        noise, noisy, act = noised(latent, col_here * 0 + (row_first + r), col_first + col_here)
        noise_keep[r] = noise
        noisy_keep[r] = noisy
        actx[r + 2, :, CH : 2 * CH] = rounded(act)

    def middles(r, carry):
        middle(r)
        return carry

    fill(FILLS[0])
    pl.semaphore_wait(barrier, len(greeted))

    def send(src, dst, send_sem, recv_sem, to):
        copy = pltpu.make_async_remote_copy(
            src_ref=src, dst_ref=dst, send_sem=send_sem, recv_sem=recv_sem,
            device_id=to, device_id_type=MESH,
        )
        copy.start()
        return copy

    rims = []
    for index, (dr, dc) in enumerate(around):
        if dc == 0:
            src = latent_ref.at[0, pl.ds(brim[dr][0], 2)]
            dst = tall.at[0 if dr > 0 else 1]
        elif dr == 0:
            src = stage.at[0 if dc < 0 else 1]
            dst = side_in.at[0 if dc > 0 else 1]
        else:
            src = stage.at[2 + (0 if dr < 0 else 2) + (0 if dc < 0 else 1)]
            dst = corner_in.at[(0 if dr > 0 else 2) + (0 if dc > 0 else 1)]
        rims.append(send(src, dst, rim_send.at[index], rim_recv.at[index], beside(dr, dc)))
    started = list(rims)

    lax.fori_loop(0, TH, middles, 0)

    lane = lax.broadcasted_iota(jnp.int32, (1, CH), 1)
    half = jnp.where(lane < CH // 2, lane, lane - CH // 2)
    angle = when * jnp.exp(f32(half) * (-math.log(10000.0)) / (CH // 2))
    wave = jnp.where(lane < CH // 2, jnp.sin(angle), jnp.cos(angle))
    wave = rounded(jnp.concatenate([wave, jnp.zeros((15, CH), jnp.float32)], axis=0))
    time_copy.wait()
    temb = jnp.dot(wave, time_ref[...], preferred_element_type=jnp.float32)[0:1]
    fill(FILLS[1])
    for copy in rims:
        copy.wait_recv()

    def outer(which, r, grid_row):
        rows = col_here * 0 + grid_row
        cols = col_first + col_here
        act = noised(tall[which, r], rows, cols)[2]
        return jnp.where(inside(rows, cols), act, 0.0)

    for which, first in ((0, -2), (1, TH)):
        for r in range(2):
            act = outer(which, r, row_first + (first + r))
            actx[first + 2 + r, :, CH : 2 * CH] = rounded(act)
    flank = lax.broadcasted_iota(jnp.int32, (16, 1), 0)
    sides = []
    for index, first in enumerate((-2, TW)):
        rows = row_first + (flank & 7)
        cols = col_first + first + shift_right(flank, 3)
        act = noised(side_in[index], rows, cols)[2]
        sides.append(jnp.where(inside(rows, cols), act, 0.0))
    corners = jnp.concatenate([f32(corner_in[index])[0:4] for index in range(4)], axis=0)
    kind = shift_right(flank, 2)
    rows = row_first + (flank & 1) + jnp.where(kind < 2, -2, TH)
    cols = col_first + (shift_right(flank, 1) & 1) + jnp.where((kind & 1) == 0, -2, TW)
    corners = jnp.where(inside(rows, cols), noised(corners, rows, cols)[2], 0.0)

    def column(side, which):
        top = corners[4 * side + 2 * which : 4 * side + 2 * which + 2]
        bottom = corners[8 + 4 * side + 2 * which : 8 + 4 * side + 2 * which + 2]
        return jnp.concatenate([top, sides[side][8 * which : 8 * which + 8], bottom], axis=0)

    centre = [f32(actx[r, :, CH : 2 * CH]) for r in range(TH + 4)]
    lefts = [column(0, 0), column(0, 1), jnp.concatenate([c[0:1] for c in centre], axis=0)]
    rights = [jnp.concatenate([c[TW - 1 : TW] for c in centre], axis=0), column(1, 0), column(1, 1)]
    for r in range(TH + 4):
        cell = centre[r]
        actx[r, :, 0:CH] = rounded(
            jnp.where(col_here == 0, lefts[1][r : r + 1], pltpu.roll(cell, 1, axis=0))
        )
        actx[r, :, 2 * CH : 3 * CH] = rounded(
            jnp.where(col_here == TW - 1, rights[1][r : r + 1], pltpu.roll(cell, TW - 1, axis=0))
        )
    for dy in range(3):
        for dx in range(3):
            both = [lefts[dx][dy : dy + 10], rights[dx][dy : dy + 10], jnp.zeros((12, CH), jnp.float32)]
            side_lhs[dy, :, dx * CH : (dx + 1) * CH] = rounded(jnp.concatenate(both, axis=0))

    total = None
    for dy in range(3):
        load(w1_ref, dy).wait()
        left = jnp.concatenate(
            [actx[dy : dy + TH + 2].reshape((TH + 2) * TW, THIRD), side_lhs[dy]], axis=0
        )
        part = jnp.dot(left, weight[dy * THIRD : (dy + 1) * THIRD], preferred_element_type=jnp.float32)
        total = part if total is None else total + part
        load(w2_ref, dy).start()
    hidden = silu(total + temb)
    flanks = hidden[(TH + 2) * TW :]
    flank = lax.broadcasted_iota(jnp.int32, (32, 1), 0)
    right_side = jnp.where(flank < 10, 0, 1)
    rows = row_first - 1 + flank - right_side * 10
    cols = col_first - 1 + right_side * (TW + 1)
    flanks = jnp.where(inside(rows, cols), flanks, 0.0)
    for r in range(TH + 2):
        cell = hidden[r * TW : (r + 1) * TW]
        if r in (0, TH + 1):
            rows = col_here * 0 + (row_first + (r - 1))
            cell = jnp.where(inside(rows, col_first + col_here), cell, 0.0)
        hid_near[r, :, CH : 2 * CH] = rounded(cell)
        hid_near[r, :, 0:CH] = rounded(
            jnp.where(col_here == 0, flanks[r : r + 1], pltpu.roll(cell, 1, axis=0))
        )
        hid_near[r, :, 2 * CH : 3 * CH] = rounded(
            jnp.where(col_here == TW - 1, flanks[10 + r : 11 + r], pltpu.roll(cell, TW - 1, axis=0))
        )

    partner = device(at, core=lax.rem(at["core"] + 1, 2))
    pair = [send(hid_near, hid_far, pair_send.at[1], pair_recv.at[1], partner)]
    fill(FILLS[2])

    total = None
    for dy in range(3):
        load(w2_ref, dy).wait()
        part = jnp.dot(
            hid_near[dy : dy + TH].reshape(TH * TW, THIRD), weight[dy * THIRD : (dy + 1) * THIRD],
            preferred_element_type=jnp.float32,
        )
        total = part if total is None else total + part
    for r in range(TH):
        full = f32(noisy_keep[r]) + total[r * TW : (r + 1) * TW]
        section_ref[0, r] = rounded(full)
        cot_near[r * TW : (r + 1) * TW] = rounded((full - noise_keep[r]) * (1.0 / math.sqrt(ROWS * COLS)))
    section_copy = pltpu.make_async_copy(section_ref, section_out, whole_sem.at[2])
    section_copy.start()
    pair.append(send(cot_near, cot_far, pair_send.at[0], pair_recv.at[0], partner))
    started += pair
    picks = [selection(third, at["core"]) for third in range(3)]

    def gather(side, cot):
        for third in range(3):
            lhs[third, side] = lax.dot_general(
                picks[third], cot[...], (((1,), (1,)), ((), ())), preferred_element_type=jnp.float32
            ).astype(jnp.bfloat16)

    gather(0, cot_near)
    for copy in pair:
        copy.wait_recv()
    gather(1, cot_far)

    def ring_one(third, level, blocks, ra, rb):
        axis = ORDERS[third][level]
        mine = at[axis]
        up = device(at, **{axis: hop(at, axis, 1)})
        down = device(at, **{axis: hop(at, axis, -1)})
        across = hop(at, axis, 2)
        sems = (third, level)
        return [
            send(blocks.at[third, across, :, pl.ds(0, CUT)], ra.at[third],
                 ring_send.at[third, level, 0], ring_recv.at[third, level, 0], up),
            send(blocks.at[third, across, :, pl.ds(CUT, THIRD - CUT)], rb.at[third],
                 ring_send.at[third, level, 1], ring_recv.at[third, level, 1], down),
            send(blocks.at[third, hop(at, axis, 1), :, pl.ds(CUT, THIRD - CUT)],
                 r1.at[third, 0, :, pl.ds(CUT, THIRD - CUT)],
                 ring_send.at[third, level, 4], ring_recv.at[third, level, 4], up),
            send(blocks.at[third, hop(at, axis, -1), :, pl.ds(0, CUT)],
                 r1.at[third, 1, :, pl.ds(0, CUT)],
                 ring_send.at[third, level, 5], ring_recv.at[third, level, 5], down),
        ]

    def ring_two(third, level, blocks, ra, rb, first, landed):
        axis = ORDERS[third][level]
        above = hop(at, axis, 1)
        below = hop(at, axis, -1)
        first[0].wait_recv()
        old = blocks[third, above, :, 0:CUT]
        blocks[third, above, :, 0:CUT] = (f32(old) + f32(ra[third])).astype(jnp.bfloat16)
        up = send(blocks.at[third, above, :, pl.ds(0, CUT)], landed.at[third, 0, :, pl.ds(0, CUT)],
                  ring_send.at[third, level, 2], ring_recv.at[third, level, 2],
                  device(at, **{axis: above}))
        first[1].wait_recv()
        old = blocks[third, below, :, CUT:THIRD]
        blocks[third, below, :, CUT:THIRD] = (f32(old) + f32(rb[third])).astype(jnp.bfloat16)
        down = send(blocks.at[third, below, :, pl.ds(CUT, THIRD - CUT)], landed.at[third, 1, :, pl.ds(CUT, THIRD - CUT)],
                    ring_send.at[third, level, 3], ring_recv.at[third, level, 3],
                    device(at, **{axis: below}))
        return [up, down]

    ones = []
    for third in range(3):
        near = hid_near[third : third + TH].reshape(TH * TW, THIRD)
        far = hid_far[third : third + TH].reshape(TH * TW, THIRD)
        total = jnp.dot(lhs[third, 0], near, preferred_element_type=jnp.float32)
        total += jnp.dot(lhs[third, 1], far, preferred_element_type=jnp.float32)
        s1[third] = rounded(total).reshape(4, 80, THIRD)
        ones.append(ring_one(third, 0, s1, r1a, r1b))
    fill(FILLS[3])
    twos = [ring_two(t, 0, s1, r1a, r1b, ones[t], r1) for t in range(3)]
    started += [copy for group in ones + twos for copy in group]
    fill(FILLS[4])
    def spread(third, level, blocks, landed, sends, recvs):
        axis = ORDERS[third][level]
        group = []
        for step in range(1, 4):
            to = hop(at, axis, step)
            group.append(
                send(blocks.at[third, to], landed.at[third, step - 1],
                     sends.at[third, step - 1], recvs.at[third, step - 1], device(at, **{axis: to}))
            )
        return group

    def gathered(third, level, blocks, landed, group):
        for copy in group:
            copy.wait_recv()
        total = f32(blocks[third, at[ORDERS[third][level]]])
        for index in range(3):
            total = total + f32(landed[third, index])
        return total

    seconds = []
    for third in range(3):
        mine = at[ORDERS[third][0]]
        for copy in twos[third] + ones[third][2:]:
            copy.wait_recv()
        total = f32(s1[third, mine]) + f32(r1[third, 0]) + f32(r1[third, 1])
        for block in range(4):
            pieces = [
                total[block * 20 : block * 20 + 20, tile * 128 : tile * 128 + 128] for tile in range(TILES)
            ]
            pieces.append(jnp.zeros((4, 128), jnp.float32))
            s2[third, block] = rounded(jnp.concatenate(pieces, axis=0))
        seconds.append(spread(third, 1, s2, r2, two_send, two_recv))
    fill(FILLS[5])
    thirds = []
    for third in range(3):
        total = gathered(third, 1, s2, r2, seconds[third])
        for block in range(4):
            pieces = []
            for tile in range(TILES):
                first = tile * 20 + block * OWN
                pieces.append(total[first : first + OWN])
            pieces.append(jnp.zeros((5, 128), jnp.float32))
            s3[third, block] = rounded(jnp.concatenate(pieces, axis=0))
        thirds.append(spread(third, 2, s3, r3, tail_send, tail_recv))
    started += [copy for group in seconds + thirds for copy in group]
    fill(PADDED)
    row[...] = jnp.zeros_like(row)
    for third in range(3):
        total = gathered(third, 2, s3, r3, thirds[third])
        for tile in range(TILES):
            for channel in range(OWN):
                lanes = pl.ds(channel * TAPS + third * THIRD + tile * 128, 128)
                row[0:1, lanes] = total[tile * OWN + channel : tile * OWN + channel + 1]

    share = project(salt, owner * RUN, row, grow, bits, acc)

    share = share * (1.0 / math.sqrt(9.0 * CH * CH))
    for slots, me, first, count in (
        (sum8, at["x"] * 2 + at["core"], 0, 7),
        (sum16, at["y"] * 4 + at["z"], 7, 15),
    ):
        slots[me] = share
        group = []
        for index in range(first, first + count):
            group.append(send(slots.at[me], slots.at[me], all_send.at[index], all_recv.at[index], peers[index]))
        for copy in group:
            copy.wait_recv()
        started += group
        share = slots[0]
        for index in range(1, count + 1):
            share = share + slots[index]
    out_ref[...] = share
    section_copy.wait()
    for copy in started:
        copy.wait_send()


def call(step, noise_seed, proj_seed, example, latent, time_weight, w1, w2):
    bf16, full = jnp.bfloat16, jnp.float32
    vmem = pltpu.VMEM
    dma = pltpu.SemaphoreType.DMA
    far = pl.BlockSpec(memory_space=pl.ANY)
    return pl.pallas_call(
        kernel,
        out_shape=(
            jax.ShapeDtypeStruct(latent.shape, bf16),
            jax.ShapeDtypeStruct((1, K), full),
        ),
        in_specs=[far] * 8,
        out_specs=(far, pl.BlockSpec(memory_space=pltpu.VMEM)),
        scratch_shapes=[
            vmem((6, 16, CH), bf16),
            vmem((2, 2, TW, CH), bf16),
            vmem((2, 16, CH), bf16),
            vmem((4, 16, CH), bf16),
            vmem((TAPS, CH), bf16),
            vmem((TH + 4, TW, THIRD), bf16),
            vmem((3, 32, THIRD), bf16),
            vmem((TH, TW, CH), full),
            vmem((TH, TW, CH), bf16),
            vmem((TH + 2, TW, THIRD), bf16),
            vmem((TH + 2, TW, THIRD), bf16),
            vmem((TH * TW, CH), bf16),
            vmem((TH * TW, CH), bf16),
            vmem((3, 2, 320, 256), bf16),
            vmem((3, 4, 80, THIRD), bf16),
            vmem((3, 80, CUT), bf16),
            vmem((3, 80, THIRD - CUT), bf16),
            vmem((3, 2, 80, THIRD), bf16),
            vmem((3, 4, 304, 128), bf16),
            vmem((3, 3, 304, 128), bf16),
            vmem((3, 4, 80, 128), bf16),
            vmem((3, 3, 80, 128), bf16),
            vmem((1, PADDED), full),
            vmem((32, PADDED), F8),
            vmem((32, K), full),
            vmem((PADDED, K), F8),
            vmem((8, 1, K), full),
            vmem((16, 1, K), full),
            pltpu.SMEM((1,), jnp.int32),
            pltpu.SMEM((1,), jnp.int32),
            pltpu.SMEM((1,), jnp.int32),
            pltpu.SMEM((1,), jnp.int32),
            dma((4,)),
            vmem(latent.shape, bf16),
            vmem(time_weight.shape, bf16),
            vmem(latent.shape, bf16),
            dma((3,)),
            dma((3,)),
            dma((8,)), dma((8,)),
            dma((2,)), dma((2,)),
            dma((3, 2, 6)), dma((3, 2, 6)),
            dma((3, 3)), dma((3, 3)),
            dma((3, 3)), dma((3, 3)),
            dma((22,)), dma((22,)),
        ],
        compiler_params=pltpu.CompilerParams(
            collective_id=0, has_side_effects=True, vmem_limit_bytes=60 * 2**20
        ),
    )(step, noise_seed, proj_seed, example, latent, time_weight, w1, w2)


def on_device(
    latent, timestep, noise_seed, proj_seed, example_ids, time_weight, conv1_weight, conv2_weight
):
    return call(
        timestep, noise_seed, proj_seed, example_ids, latent, time_weight, conv1_weight, conv2_weight
    )


def solution(mesh):
    placed = (P(None, "row", "col", None), P(), P(), P(), P(), P(), P(), P())
    return jax.shard_map(
        on_device,
        mesh=mesh,
        in_specs=placed,
        out_specs=(P(None, "row", "col", None), P()),
        check_vma=False,
    )
```
